128 devices in a mesh: section: 4 (over z), expert: 4 (over y), dp: 8 (over x, core).
Axes of the slice: x: 4, y: 4, z: 4, core: 2. Of those that a mesh axis runs over, the one named last changes fastest.
Arguments:
- tokens: bfloat16 [2, 2048, 2048], P(None, ('expert', 'dp')), may hold values from -24 to 24
- expert_ids: int32 [4, 2, 2048, 4], P('section', None, ('expert', 'dp')), may hold values from 0 to 31, all different within a row; in each aligned block of 64 rows (0 to 63, 64 to 127, ..., all dimensions but the last counted through in order) at most 16 rows name the same one
- labels: int32 [2, 2048], P(None, ('expert', 'dp')), may hold values from 0 to 127
- router: bfloat16 [4, 2048, 32], P('section'), may hold values from -0.125 to 0.125
- class_head: bfloat16 [2048, 128], replicated, may hold values from -0.5 to 0.5
- w_gate: bfloat16 [4, 32, 2048, 768], P('section', ('expert', 'dp')), may hold values from -0.125 to 0.125
- w_up: bfloat16 [4, 32, 2048, 768], P('section', ('expert', 'dp')), may hold values from -0.125 to 0.125
- w_down: bfloat16 [4, 32, 768, 2048], P('section', ('expert', 'dp')), may hold values from -0.21875 to 0.21875
Outputs:
- mean_loss: float32 [], replicated
- grad_head: float32 [2048, 128], replicated
- grad_router: float32 [4, 2048, 32], P('section')
- grad_gate: bfloat16 [4, 32, 2048, 768], P('section', ('expert', 'dp'))
- grad_up: bfloat16 [4, 32, 2048, 768], P('section', ('expert', 'dp'))
- grad_down: bfloat16 [4, 32, 768, 2048], P('section', ('expert', 'dp'))
The draws below stay inside these ranges and needn't reach their ends.
Inputs may be any that keep to these rules, and one draw needn't show every extreme that they name: `expert_ids`: each token names 4 different experts; among the 64 tokens of one device in one micro-batch and layer no expert is named more than 16 times, a bound that some block reaches.
All inputs are finite; a program needn't handle non-finite values.
Results may differ from the reference program's by a relative error of at most 0.025.
Values may be sent and summed in bfloat16 or wider, within the bound.
No kernel may reach another device: no remote copies, remote signals or barrier semaphores. Data moves between devices by JAX's collectives and lax.ppermute only.
A program may use at most 320 MiB of HBM per device.

```python
import math
import jax
import jax.numpy as jnp
import numpy as np
from jax import lax

D = 2048
FFE = 768
NCLASS = 128
TOPK = 4
MB = 2
TOK_MB = 64
EXPERTS = 32
TOKENS = 2048
CAP = 16
N_SECTION = 4


def draw_tokens(key, part):
    key_cols, key_rows, key_base = jax.random.split(key, 3)
    col_scale = jnp.exp(jax.random.uniform(key_cols, (1, 1, D), jnp.float32, math.log(0.3), math.log(3.0)))
    row_scale = jnp.exp(jax.random.uniform(key_rows, (MB, TOKENS, 1), jnp.float32, math.log(0.5), math.log(2.0)))
    base_draw = jax.random.normal(key_base, (MB, TOKENS, D), jnp.float32)
    return jnp.clip(base_draw * row_scale * col_scale, -24.0, 24.0).astype(jnp.bfloat16)


def with_ends(values, rng, smallest, high):
    extent = values.shape
    place = [jax.random.randint(jax.random.fold_in(rng, axis), (), 0, extent[axis]) for axis in range(len(extent))]
    values = values.at[tuple(place)].set(smallest)
    longest = extent.index(max(extent))
    place[longest] = (place[longest] + 1) % extent[longest]
    return values.at[tuple(place)].set(high)


def block_levels(stream_key, shape, pieces, least, largest):
    def one(position, blocks):
        draws = jax.random.uniform(jax.random.fold_in(jax.random.fold_in(stream_key, 6), position), (blocks,), jnp.float32, least / len(pieces), largest / len(pieces))
        return jnp.repeat(jnp.exp(draws), shape[position] // blocks).reshape((-1,) + (1,) * (len(shape) - position - 1))

    loudness = one(*pieces[0])
    for cut in pieces[1:]:
        loudness = loudness * one(*cut)
    return loudness


def deal_out(own_key, own, number, rows, count, top, most, slope):
    ranking = jax.random.permutation(own_key, count)
    crowded, common = portions_of(count, rows * top, most, slope, True), portions_of(count, rows * top, most, slope, False)
    places = jnp.arange(count)

    def named(lengths, rotation):
        used = int((lengths > 0).sum())
        fixed = max(1, used // 4)
        shifted = fixed + (places - fixed + rotation * (used - fixed)) % max(1, count - fixed)
        return jnp.zeros((count,), jnp.int32).at[ranking[jnp.where(places < fixed, places, shifted)]].set(jnp.asarray(lengths, jnp.int32))

    lengths = jnp.where(number % 4 == 0, named(crowded, number // 4), named(common, number - number // 4 - 1))
    mixed = jax.random.permutation(jax.random.fold_in(own, 3), count)
    source_of, taker = mixed[0:count // 2 * 2:2], mixed[1:count // 2 * 2:2]
    margin = jnp.minimum(lengths[source_of] - 1, most - lengths[taker]) // 2
    margin = jnp.where((source_of == ranking[0]) | (taker == ranking[0]) | (lengths[taker] == 0), 0, jnp.maximum(margin, 0))
    shifted = jax.random.randint(jax.random.fold_in(own, 4), (count // 2,), 0, 1 << 20) % (margin + 1)
    lengths = lengths.at[source_of].add(-shifted).at[taker].add(shifted)
    items = jnp.searchsorted(jnp.cumsum(lengths), jnp.arange(rows * top), side="right").astype(jnp.int32)
    table = items.reshape(top, rows).T
    table = table[jax.random.permutation(jax.random.fold_in(own, 1), rows)]
    rotation = jax.random.randint(jax.random.fold_in(own, 2), (rows, 1), 0, top)
    return jnp.take_along_axis(table, (jnp.arange(top)[None, :] + rotation) % top, axis=1)


def portions_of(number_of, total, bound, slope, full):
    weights = [(1 << 20) // math.isqrt(standing ** slope) + 1 for standing in range(1, number_of + 1)]
    largest = bound if full else min(bound, max(-(-total // number_of), total * weights[0] // sum(weights)))
    least = 1 if total - largest >= number_of - 1 else 0
    holding, spare = [largest] + [least] * (number_of - 1), total - largest - least * (number_of - 1)
    while spare > 0:
        candidates = [i for i in range(1, number_of) if holding[i] < largest] or [i for i in range(1, number_of) if holding[i] < bound]
        pool, remaining = sum([weights[i] for i in candidates]), spare
        for i in candidates:
            extra = min(bound - holding[i], max(1, remaining * weights[i] // pool), spare)
            holding[i] = holding[i] + extra
            spare = spare - extra
    return np.array(holding)


def scatter_about(own_key, shape, scale, most, pieces=(), kind=jnp.bfloat16):
    gain = block_levels(own_key, shape, pieces, -0.22, 0.18) if pieces else 1.0
    result = jax.random.normal(own_key, shape, jnp.float32) * scale * gain
    return jnp.minimum(jnp.maximum(result, -most), most).astype(kind)


def setup_inputs(seed: int = 0) -> dict:
    seeds = jax.random.split(jax.random.key(seed), 9)
    tokens = draw_tokens(jax.random.fold_in(seeds[8], 71), 0)
    expert_ids_keys = jax.random.split(jax.random.fold_in(seeds[1], 1), N_SECTION * MB * TOKENS // TOK_MB)
    expert_ids_turns = jax.random.permutation(jax.random.fold_in(seeds[1], 3), N_SECTION * MB * TOKENS // TOK_MB)
    expert_ids = jax.vmap(lambda own, number: deal_out(jax.random.fold_in(seeds[1], 2), own, number, TOK_MB, EXPERTS, TOPK, CAP, 2))(expert_ids_keys, expert_ids_turns).reshape((N_SECTION, MB, TOKENS, TOPK))
    labels = with_ends(jax.random.randint(seeds[2], (MB, TOKENS), 0, NCLASS), jax.random.fold_in(seeds[2], 1), 0, NCLASS - 1).astype(jnp.int32)
    router = scatter_about(seeds[3], (N_SECTION, D, EXPERTS), D ** -0.5, 0.125, ((0, 4),))
    class_head = scatter_about(seeds[4], (D, NCLASS), (D // 16) ** -0.5, 0.5)
    w_gate = scatter_about(seeds[5], (N_SECTION, EXPERTS, D, FFE), D ** -0.5, 0.125, ((0, 4), (1, 32)))
    w_up = scatter_about(seeds[6], (N_SECTION, EXPERTS, D, FFE), D ** -0.5, 0.125, ((0, 4), (1, 32)))
    w_down = scatter_about(seeds[7], (N_SECTION, EXPERTS, FFE, D), FFE ** -0.5, 0.21875, ((0, 4), (1, 32)))
    return dict(tokens=tokens, expert_ids=expert_ids, labels=labels, router=router, class_head=class_head, w_gate=w_gate, w_up=w_up, w_down=w_down)


soft_cap = 30.0
norm_eps = 1e-06

def capped(values):
    return soft_cap * jnp.tanh(values / soft_cap)

def normalize(layer_in):
    hidden_f = layer_in.astype(jnp.float32)
    inv_rms = lax.rsqrt(lax.optimization_barrier(jnp.mean(hidden_f * hidden_f, axis=-1, keepdims=True)) + norm_eps)
    return (hidden_f, inv_rms, (hidden_f * inv_rms).astype(jnp.bfloat16))

def gate_probs(normed, ids_now, router_w):
    logits = jnp.dot(normed, router_w, preferred_element_type=jnp.float32)
    one_hot = (ids_now[:, :, None] == jnp.arange(router_w.shape[1], dtype=jnp.int32)[None, None, :]).astype(jnp.float32)
    chosen = capped(lax.optimization_barrier(jnp.sum(one_hot * logits[:, None, :], axis=-1)))
    weights = jnp.exp(chosen)
    return (one_hot, chosen, weights / lax.optimization_barrier(jnp.sum(weights, axis=-1, keepdims=True)))

def expert_lists(flat_ids):

    def pick_rows(expert):
        return jnp.nonzero(flat_ids == expert, size=CAP * EXPERTS, fill_value=flat_ids.shape[0])[0].astype(jnp.int32)
    return lax.map(pick_rows, jnp.arange(EXPERTS, dtype=jnp.int32))

def contract_first(left, right):
    return lax.dot_general(left, right, (((0,), (0,)), ((), ())), preferred_element_type=jnp.float32)

def contract_last(left, right):
    return lax.dot_general(left, right, (((1,), (1,)), ((), ())), preferred_element_type=jnp.float32)

def moe_forward(layer_in, ids_now, router_w, gate_w, up_w, down_w):
    hidden_f, inv_rms, normed = normalize(layer_in)
    one_hot, chosen, probs = gate_probs(normed, ids_now, router_w)
    row_total = ids_now.shape[0] * TOPK
    row_lists = expert_lists(ids_now.reshape(-1))

    def one_expert(operands):
        picked, gate_e, up_e, down_e = operands
        tile_in = normed[jnp.minimum(picked, row_total - 1) // TOPK]
        gate_act = jnp.dot(tile_in, gate_e, preferred_element_type=jnp.float32)
        up_act = jnp.dot(tile_in, up_e, preferred_element_type=jnp.float32)
        hidden_act = (gate_act * jax.nn.sigmoid(gate_act) * up_act).astype(jnp.bfloat16)
        return jnp.dot(hidden_act, down_e, preferred_element_type=jnp.float32).astype(jnp.bfloat16)
    results = lax.map(one_expert, (row_lists, gate_w, up_w, down_w))
    expert_out = jnp.zeros((row_total, D), jnp.bfloat16).at[row_lists.reshape(-1)].set(results.reshape(-1, D), mode='drop')
    expert_out = expert_out.reshape(-1, TOPK, D)
    layer_out = (hidden_f + lax.optimization_barrier(jnp.sum(probs[:, :, None] * expert_out.astype(jnp.float32), axis=1))).astype(jnp.bfloat16)
    return (layer_out, expert_out)

def moe_backward(grad_out, layer_in, expert_out, ids_now, router_w, gate_w, up_w, down_w):
    hidden_f, inv_rms, normed = normalize(layer_in)
    one_hot, chosen, probs = gate_probs(normed, ids_now, router_w)
    grad_f = grad_out.astype(jnp.float32)
    grad_prob = lax.optimization_barrier(jnp.sum(grad_f[:, None, :] * expert_out.astype(jnp.float32), axis=-1))
    grad_rows = (probs[:, :, None] * grad_f[:, None, :]).astype(jnp.bfloat16).reshape(-1, D)
    row_total = grad_rows.shape[0]
    row_lists = expert_lists(ids_now.reshape(-1))

    def one_expert(operands):
        picked, gate_e, up_e, down_e = operands
        is_valid = (picked < row_total)[:, None]
        safe_rows = jnp.minimum(picked, row_total - 1)
        tile_in = jnp.where(is_valid, normed[safe_rows // TOPK], jnp.zeros((), jnp.bfloat16))
        tile_grad = jnp.where(is_valid, grad_rows[safe_rows], jnp.zeros((), jnp.bfloat16))
        gate_act = jnp.dot(tile_in, gate_e, preferred_element_type=jnp.float32)
        up_act = jnp.dot(tile_in, up_e, preferred_element_type=jnp.float32)
        sigmoid_gate = jax.nn.sigmoid(gate_act)
        silu_gate = gate_act * sigmoid_gate
        hidden_act = (silu_gate * up_act).astype(jnp.bfloat16)
        grad_down_e = contract_first(hidden_act, tile_grad)
        grad_hidden = contract_last(tile_grad, down_e)
        grad_gate_act = (grad_hidden * up_act * sigmoid_gate * (1.0 + gate_act * (1.0 - sigmoid_gate))).astype(jnp.bfloat16)
        grad_up_act = (grad_hidden * silu_gate).astype(jnp.bfloat16)
        grad_gate_e = contract_first(tile_in, grad_gate_act)
        grad_up_e = contract_first(tile_in, grad_up_act)
        grad_in_rows = (contract_last(grad_gate_act, gate_e) + contract_last(grad_up_act, up_e)).astype(jnp.bfloat16)
        return (grad_gate_e, grad_up_e, grad_down_e, grad_in_rows)
    grad_gate, grad_up, grad_down, grad_in_rows = lax.map(one_expert, (row_lists, gate_w, up_w, down_w))
    grad_parts = jnp.zeros((row_total, D), jnp.bfloat16).at[row_lists.reshape(-1)].set(grad_in_rows.reshape(-1, D), mode='drop')
    grad_parts = grad_parts.reshape(-1, TOPK, D)
    scaled = chosen / soft_cap
    grad_chosen = probs * (grad_prob - lax.optimization_barrier(jnp.sum(probs * grad_prob, axis=-1, keepdims=True))) * (1.0 - scaled * scaled)
    grad_route = lax.optimization_barrier(jnp.sum(grad_chosen[:, :, None] * one_hot, axis=1)).astype(jnp.bfloat16)
    grad_router = contract_first(normed, grad_route)
    grad_normed = lax.optimization_barrier(jnp.sum(grad_parts.astype(jnp.float32), axis=1)) + contract_last(grad_route, router_w)
    normed_f = hidden_f * inv_rms
    grad_in = (grad_f + inv_rms * (grad_normed - normed_f * lax.optimization_barrier(jnp.mean(grad_normed * normed_f, axis=-1, keepdims=True)))).astype(jnp.bfloat16)
    return (grad_in, grad_router, grad_gate, grad_up, grad_down)

def reference(tokens, expert_ids, labels, router, class_head, w_gate, w_up, w_down):
    section_inputs = []
    section_outputs = []
    finals = []
    for micro_num in range(MB):
        layer_in = tokens[micro_num]
        saved_in = []
        saved_out = []
        for section_num in range(N_SECTION):
            saved_in.append(layer_in)
            layer_in, expert_out = moe_forward(layer_in, expert_ids[section_num, micro_num], router[section_num], w_gate[section_num], w_up[section_num], w_down[section_num])
            saved_out.append(expert_out)
        section_inputs.append(saved_in)
        section_outputs.append(saved_out)
        finals.append(layer_in)
    final_rows = jnp.stack(finals).reshape(-1, D)
    class_logits = capped(jnp.dot(final_rows, class_head, preferred_element_type=jnp.float32))
    class_weights = jnp.exp(class_logits)
    class_total = lax.optimization_barrier(jnp.sum(class_weights, axis=-1, keepdims=True))
    label_hot = (labels.reshape(-1)[:, None] == jnp.arange(NCLASS, dtype=jnp.int32)[None, :]).astype(jnp.float32)
    mean_loss = jnp.mean(jnp.log(class_total[:, 0]) - lax.optimization_barrier(jnp.sum(label_hot * class_logits, axis=-1)))
    scaled = class_logits / soft_cap
    grad_logits = ((class_weights / class_total - label_hot) * (1.0 - scaled * scaled)).astype(jnp.bfloat16)
    grad_head = contract_first(final_rows, grad_logits)
    grad_top = contract_last(grad_logits, class_head).astype(jnp.bfloat16).reshape(MB, -1, D)
    grad_list = [grad_top[micro_num] for micro_num in range(MB)]
    router_list = []
    gate_list = []
    up_list = []
    down_list = []
    for section_num in reversed(range(N_SECTION)):
        router_sum = jnp.zeros((D, EXPERTS), jnp.float32)
        gate_sum = jnp.zeros((EXPERTS, D, FFE), jnp.float32)
        up_sum = jnp.zeros((EXPERTS, D, FFE), jnp.float32)
        down_sum = jnp.zeros((EXPERTS, FFE, D), jnp.float32)
        for micro_num in range(MB):
            grad_cur, grad_r, grad_g, grad_u, grad_d = moe_backward(grad_list[micro_num], section_inputs[micro_num][section_num], section_outputs[micro_num][section_num], expert_ids[section_num, micro_num], router[section_num], w_gate[section_num], w_up[section_num], w_down[section_num])
            grad_list[micro_num] = grad_cur
            router_sum = router_sum + grad_r
            gate_sum = gate_sum + grad_g
            up_sum = up_sum + grad_u
            down_sum = down_sum + grad_d
        router_list.append(router_sum)
        gate_list.append(gate_sum.astype(jnp.bfloat16))
        up_list.append(up_sum.astype(jnp.bfloat16))
        down_list.append(down_sum.astype(jnp.bfloat16))
    grad_router = jnp.stack(router_list[::-1])
    grad_gate = jnp.stack(gate_list[::-1])
    grad_up = jnp.stack(up_list[::-1])
    grad_down = jnp.stack(down_list[::-1])
    return (mean_loss, grad_head, grad_router, grad_gate, grad_up, grad_down)
```

```python
import functools

import jax
import jax.numpy as jnp
from jax import lax
from jax.experimental import pallas as pl
from jax.experimental.pallas import tpu as pltpu
from jax.sharding import PartitionSpec as P

soft_cap = 30.0
norm_eps = 1e-06
BF = jnp.bfloat16
F32 = jnp.float32
plane = ("expert", "dp")
MIB = 1 << 20


def dot(left, right, dims):
    return lax.dot_general(left, right, (dims, ((), ())), preferred_element_type=F32)


def nn(left, right):
    return dot(left, right, ((1,), (0,)))


def nt(left, right):
    return dot(left, right, ((1,), (1,)))


def tn(left, right):
    return dot(left, right, ((0,), (0,)))


def sds(shape, dtype):
    return jax.ShapeDtypeStruct(shape, dtype)


def whole(array):
    rank = len(array.shape)
    return pl.BlockSpec(array.shape, lambda *_: (0,) * rank)


def run(kernel, args, in_specs, outs, out_specs, grid=(1,), scratch=(), aliases=None, cost=1e9):
    moved = sum(a.size * a.dtype.itemsize for a in args[1:])
    return pl.pallas_call(
        kernel,
        grid_spec=pltpu.PrefetchScalarGridSpec(
            num_scalar_prefetch=1,
            grid=grid,
            in_specs=in_specs,
            out_specs=out_specs,
            scratch_shapes=list(scratch),
        ),
        out_shape=outs,
        input_output_aliases=aliases or {},
        compiler_params=pltpu.CompilerParams(vmem_limit_bytes=40 * MIB),
        cost_estimate=pl.CostEstimate(flops=int(cost), bytes_accessed=moved, transcendentals=0),
    )(*args)


def normalize(layer_in):
    hidden_f = layer_in.astype(F32)
    inv_rms = lax.rsqrt(jnp.mean(hidden_f * hidden_f, axis=-1, keepdims=True) + norm_eps)
    return hidden_f, inv_rms, (hidden_f * inv_rms).astype(BF)


def hi_lo(values):
    high = values.astype(BF)
    return high, (values - high.astype(F32)).astype(BF)


def spreading(experts, slots):
    shape = (experts, experts * slots)
    column = lax.broadcasted_iota(jnp.int32, shape, 1)
    row = lax.broadcasted_iota(jnp.int32, shape, 0)
    return ((column // slots) == row).astype(F32).astype(BF)


def pick(flag, refs):
    if len(refs) == 1:
        return refs[0][...]
    return jnp.where(flag, refs[0][...], refs[1][...])


def place_kernel(slots, sec, ids_ref, pt_ref):
    micros, rows, width = pt_ref.shape
    column = lax.broadcasted_iota(jnp.int32, (rows, width), 1)
    expert = column // slots
    slot = (column - expert * slots).astype(F32)
    below = (
        lax.broadcasted_iota(jnp.int32, (rows, rows), 0)
        > lax.broadcasted_iota(jnp.int32, (rows, rows), 1)
    ).astype(F32).astype(BF)
    for micro in range(micros):
        ids = ids_ref[micro]
        named = jnp.zeros((rows, width), F32)
        for k in range(ids.shape[1]):
            named = named + (ids[:, k : k + 1] == expert).astype(F32)
        before = nn(below, named.astype(BF))
        here = (named > 0.5) & (before == slot)
        pt_ref[micro] = here.astype(F32).astype(BF)


def prep_fwd_kernel(both, sec, *refs):
    ins, (pt_ref, h_ref, n_ref, out_ref) = refs[:-4], refs[-4:]
    step = pl.program_id(0)
    chunk = out_ref.shape[1]

    @pl.when(step == 0)
    def _():
        layer_in = pick(sec[0] == 0, ins)
        h_ref[...] = layer_in
        n_ref[...] = normalize(layer_in)[2]

    cols = n_ref[:, pl.ds(pl.multiple_of(step * chunk, chunk), chunk)]
    out_ref[...] = tn(pt_ref[0], cols).astype(BF)


def route_fwd_kernel(slots, sec, n_ref, router_ref, pt_ref, phl_ref, p_ref, c2_ref):
    logits = nn(n_ref[...], router_ref[...])
    spread = spreading(logits.shape[1], slots)
    high, low = hi_lo(logits)
    lowest = (logits - high.astype(F32) - low.astype(F32)).astype(BF)
    wide = nn(high, spread) + nn(low, spread) + nn(lowest, spread)
    tanh = jnp.tanh(wide / soft_cap)
    weights = pt_ref[0].astype(F32) * jnp.exp(soft_cap * tanh)
    probs = weights / jnp.sum(weights, axis=-1, keepdims=True)
    high, low = hi_lo(probs)
    rows = probs.shape[0]
    phl_ref[:rows] = high
    phl_ref[rows:] = low
    p_ref[...] = probs
    c2_ref[...] = 1.0 - tanh * tanh


def expert_fwd_kernel(sec, x_ref, wg_ref, wu_ref, wd_ref, out_ref, acc_ref):
    step = pl.program_id(0)
    packed = x_ref[...]
    gate = nn(packed, wg_ref[...])
    up = nn(packed, wu_ref[...])
    hidden = (gate * jax.nn.sigmoid(gate) * up).astype(BF)
    part = nn(hidden, wd_ref[...])

    @pl.when(step == 0)
    def _():
        acc_ref[...] = part

    @pl.when((step > 0) & (step < pl.num_programs(0) - 1))
    def _():
        acc_ref[...] += part

    @pl.when(step == pl.num_programs(0) - 1)
    def _():
        out_ref[...] = (acc_ref[...] + part).astype(BF)


def combine_fwd_kernel(sec, ret_ref, h_ref, phl_ref, out_ref):
    rows = h_ref.shape[0]
    both = nn(phl_ref[...], ret_ref[...])
    out_ref[...] = (h_ref[...].astype(F32) + (both[:rows] + both[rows:])).astype(BF)


def head_kernel(sec, final_ref, head_ref, label_ref, gtop_ref, glog_ref, loss_ref):
    class_logits = soft_cap * jnp.tanh(nn(final_ref[...], head_ref[...]) / soft_cap)
    weights = jnp.exp(class_logits)
    total = jnp.sum(weights, axis=-1, keepdims=True)
    hot = (lax.broadcasted_iota(jnp.int32, weights.shape, 1) == label_ref[...]).astype(F32)
    token_loss = jnp.log(total) - jnp.sum(hot * class_logits, axis=-1, keepdims=True)
    scaled = class_logits / soft_cap
    glog = ((weights / total - hot) * (1.0 - scaled * scaled)).astype(BF)
    glog_ref[...] = glog
    gtop_ref[...] = nt(glog, head_ref[...]).astype(BF)
    loss_ref[...] = jnp.broadcast_to(jnp.sum(token_loss, axis=0, keepdims=True), loss_ref.shape)


def prep_bwd_kernel(tick, n_g, n_p, sec, *refs):
    g_refs, phl_refs, (g_ref, out_ref) = refs[:n_g], refs[n_g : n_g + n_p], refs[n_g + n_p :]
    flag = sec[0] == sec[1] - tick
    step = pl.program_id(0)
    chunk = out_ref.shape[1]

    @pl.when(step == 0)
    def _():
        g_ref[...] = pick(flag, g_refs)

    cols = g_ref[:, pl.ds(pl.multiple_of(step * chunk, chunk), chunk)]
    probs = pick(flag, phl_refs)
    out_ref[...] = tn(probs, jnp.concatenate([cols, cols], axis=0)).astype(BF)


def route_bwd_kernel(tick, slots, n, micros, sec, g_ref, *refs):
    r_refs, h_refs, p_refs, c_refs = (refs[i * n : (i + 1) * n] for i in range(4))
    router_t_ref, acc_in_ref, gn_ref, acc_ref = refs[4 * n :]
    flag = sec[0] == sec[1] - tick
    micro = tick - (sec[1] - 1 - sec[0])
    active = (micro >= 0) & (micro < micros)
    grad = g_ref[...]
    grad_prob = nt(grad, pick(flag, r_refs))
    probs = pick(flag, p_refs)
    mean = jnp.sum(probs * grad_prob, axis=-1, keepdims=True)
    grad_chosen = (probs * (grad_prob - mean) * pick(flag, c_refs)).astype(BF)
    experts = router_t_ref.shape[0]
    grad_route = nt(grad_chosen, spreading(experts, slots)).astype(BF)
    gn_ref[...] = nn(grad_route, router_t_ref[...])
    normed = normalize(pick(flag, h_refs))[2]
    acc_ref[...] = acc_in_ref[...] + jnp.where(active, tn(grad_route, normed), 0.0)


def again_kernel(tick, n, sec, *refs):
    x_refs = refs[:n]
    wg_ref, wu_ref = refs[n : n + 2]
    a1_ref, a2_ref, ht_ref, xt_ref = refs[-4:]
    packed = pick(sec[0] == sec[1] - tick, x_refs)
    gate = nn(packed, wg_ref[...])
    up = nn(packed, wu_ref[...])
    sigmoid = jax.nn.sigmoid(gate)
    silu = gate * sigmoid
    a1_ref[...] = up * sigmoid * (1.0 + gate * (1.0 - sigmoid))
    a2_ref[...] = silu
    ht_ref[0] = (silu * up).astype(BF).T

    @pl.when(pl.program_id(0) == 0)
    def _():
        xt_ref[0] = packed.T


def expert_bwd_kernel(last, sec, dy_ref, wd_ref, a1_ref, a2_ref, *refs):
    step = pl.program_id(0)
    if last:
        gg_ref, gu_ref, dys_ref = refs[-3:]
    else:
        wg_ref, wu_ref = refs[:2]
        gg_ref, gu_ref, dys_ref, out_ref, acc_ref = refs[-5:]
    rows = dy_ref[...]
    grad_hidden = nt(rows, wd_ref[...])
    gg = (grad_hidden * a1_ref[...]).astype(BF)
    gu = (grad_hidden * a2_ref[...]).astype(BF)
    gg_ref[0] = gg
    gu_ref[0] = gu

    @pl.when(step == 0)
    def _():
        dys_ref[0] = rows

    if last:
        return
    part = nt(gg, wg_ref[...]) + nt(gu, wu_ref[...])

    @pl.when(step == 0)
    def _():
        acc_ref[...] = part

    @pl.when((step > 0) & (step < pl.num_programs(0) - 1))
    def _():
        acc_ref[...] += part

    @pl.when(step == pl.num_programs(0) - 1)
    def _():
        out_ref[...] = (acc_ref[...] + part).astype(BF)


def combine_bwd_kernel(tick, n, sec, ret_ref, pt_ref, gn_ref, g_ref, *refs):
    h_refs, (out_ref, sum_ref) = refs[:n], refs[n:]
    step = pl.program_id(0)
    chunk = ret_ref.shape[1]
    cols = pl.ds(pl.multiple_of(step * chunk, chunk), chunk)
    sum_ref[:, cols] = nn(pt_ref[0], ret_ref[...])

    @pl.when(step == pl.num_programs(0) - 1)
    def _():
        hidden_f, inv_rms, _ = normalize(pick(sec[0] == sec[1] - tick, h_refs))
        grad_normed = sum_ref[...] + gn_ref[...]
        normed_f = hidden_f * inv_rms
        mean = jnp.mean(grad_normed * normed_f, axis=-1, keepdims=True)
        out_ref[...] = (
            g_ref[...].astype(F32) + inv_rms * (grad_normed - normed_f * mean)
        ).astype(BF)


def weights_kernel(sec, xt_ref, gg_ref, gu_ref, ht_ref, dy_ref, gate_ref, up_ref, down_ref):
    gate_ref[...] = (nn(xt_ref[0], gg_ref[0]) + nn(xt_ref[1], gg_ref[1])).astype(BF)
    up_ref[...] = (nn(xt_ref[0], gu_ref[0]) + nn(xt_ref[1], gu_ref[1])).astype(BF)
    down_ref[...] = (nn(ht_ref[0], dy_ref[0]) + nn(ht_ref[1], dy_ref[1])).astype(BF)


def to_owners(rows):
    return lax.all_to_all(rows, plane, split_axis=0, concat_axis=0, tiled=True)


def from_behind(block, axis, distance):
    devices = range(lax.axis_size(axis))
    route = [(i - distance, i) for i in devices if i - distance in devices]
    return lax.ppermute(block, axis, route)


def shards(tokens, expert_ids, labels, router, class_head, w_gate, w_up, w_down):
    sections = lax.axis_size("section")
    section = lax.axis_index("section")
    experts = lax.axis_size(plane)
    micros, rows, width = tokens.shape
    top = expert_ids.shape[3]
    slots = 2 * rows * top // experts
    packed = experts * slots
    router_w = router[0]
    router_t = router_w.T
    gate_w, up_w, down_w = w_gate[0, 0], w_up[0, 0], w_down[0, 0]
    ffe = gate_w.shape[1]
    ticks = micros + sections - 1
    sec = jnp.stack([section, jnp.int32(sections)]).astype(jnp.int32)
    tile = 256
    chunk = 512
    steps = ffe // tile
    col_steps = width // chunk
    row_block = pl.BlockSpec((rows, chunk), lambda i, s: (0, i))
    buf_block = pl.BlockSpec((packed, chunk), lambda i, s: (0, i))
    in_block = pl.BlockSpec((width, tile), lambda i, s: (0, i))
    down_block = pl.BlockSpec((tile, width), lambda i, s: (i, 0))
    act_block = pl.BlockSpec((packed, tile), lambda i, s: (0, i))
    row_full = sds((rows, width), BF)
    buf_full = sds((packed, width), BF)
    matmul = 2.0 * packed * width * ffe

    [places] = run(
        functools.partial(place_kernel, slots),
        (sec, expert_ids[0]),
        [whole(expert_ids[0])],
        [sds((micros, rows, packed), BF)],
        [whole(sds((micros, rows, packed), BF))],
    )

    def place_block(micro_of):
        return pl.BlockSpec(
            (1, rows, packed), lambda i, s: (jnp.clip(micro_of(s), 0, micros - 1), 0, 0)
        )

    saved = []
    finals = []
    incoming = None
    for tick in range(ticks):
        if tick == 0:
            ins = (tokens[0],)
        elif tick < micros:
            ins = (tokens[tick], incoming)
        else:
            ins = (incoming,)
        micro_spec = place_block(lambda s, tick=tick: tick - s[0])
        layer_in, normed, outgoing = run(
            functools.partial(prep_fwd_kernel, len(ins) == 2),
            (sec, *ins, places),
            [whole(row_full)] * len(ins) + [micro_spec],
            [row_full, row_full, buf_full],
            [whole(row_full), whole(row_full), buf_block],
            grid=(col_steps,),
            cost=2 * rows * packed * width,
        )
        arrived = to_owners(outgoing)
        wide = sds((rows, packed), F32)
        two = sds((2 * rows, packed), BF)
        probs_two, probs, slope = run(
            functools.partial(route_fwd_kernel, slots),
            (sec, normed, router_w, places),
            [whole(row_full), whole(router_w), micro_spec],
            [two, wide, wide],
            [whole(two), whole(wide), whole(wide)],
            cost=2 * rows * width * experts,
        )
        [results] = run(
            expert_fwd_kernel,
            (sec, arrived, gate_w, up_w, down_w),
            [whole(buf_full), in_block, in_block, down_block],
            [buf_full],
            [whole(buf_full)],
            grid=(steps,),
            scratch=[pltpu.VMEM((packed, width), F32)],
            cost=3 * matmul,
        )
        returned = to_owners(results)
        [layer_out] = run(
            combine_fwd_kernel,
            (sec, returned, layer_in, probs_two),
            [buf_block, row_block, whole(two)],
            [row_full],
            [row_block],
            grid=(col_steps,),
            cost=4 * rows * packed * width,
        )
        saved.append((arrived, returned, layer_in, probs_two, probs, slope))
        if tick + 1 < ticks:
            incoming = from_behind(layer_out, "section", 1)
        micro = tick - (sections - 1)
        if micro >= 0:
            label_col = labels[micro][:, None]
            glog_full, loss_full = sds((rows, class_head.shape[1]), BF), sds((8, 128), F32)
            finals.append(
                (
                    layer_out,
                    *run(
                        head_kernel,
                        (sec, layer_out, class_head, label_col),
                        [whole(row_full), whole(class_head), whole(label_col)],
                        [row_full, glog_full, loss_full],
                        [whole(row_full), whole(glog_full), whole(loss_full)],
                        cost=4 * rows * width * class_head.shape[1],
                    ),
                )
            )

    head_term = sum(
        dot(final, glog, ((0,), (0,))) for final, _, glog, _ in finals
    )
    loss_term = sum(loss for _, _, _, loss in finals)
    share = width // experts
    head_parts = jnp.concatenate(
        [
            head_term.reshape(experts, share, -1),
            jnp.broadcast_to(loss_term[None], (experts, *loss_term.shape)),
        ],
        axis=1,
    )
    head_parts = lax.psum_scatter(head_parts, plane, scatter_dimension=0, tiled=True)
    head_all = lax.all_gather(head_parts, ("section", *plane), axis=0, tiled=True)
    head_all = head_all[(sections - 1) * experts :]
    head_total = head_all[:, :share].reshape(width, -1)
    mean_loss = head_all[0, share, 0] / (micros * rows * experts)

    router_sum = jnp.zeros((experts, width), F32)
    store = None
    for tick in range(ticks):
        at = [
            s_num + tick - (sections - 1 - s_num)
            for s_num in reversed(range(sections))
            if 0 <= tick - (sections - 1 - s_num) < micros
        ]
        cands = [saved[t] for t in at]
        if tick == 0:
            grads = (finals[0][1],)
        elif tick < micros:
            grads = (finals[tick][1], incoming)
        else:
            grads = (incoming,)
        micro_of = lambda s, tick=tick: tick - (s[1] - 1 - s[0])
        last = tick + 1 == ticks

        def slot_block(shape, place, micro_of=micro_of):
            def index(i, s):
                micro = micro_of(s)
                return (jnp.where((micro >= 0) & (micro < micros), micro, micros), *place(i))

            return pl.BlockSpec((1, *shape), index)

        count = len(cands)
        gsel, outgoing = run(
            functools.partial(prep_bwd_kernel, tick, len(grads), count),
            (sec, *grads, *[c[3] for c in cands]),
            [whole(row_full)] * len(grads) + [whole(c[3]) for c in cands],
            [row_full, buf_full],
            [whole(row_full), buf_block],
            grid=(col_steps,),
            cost=4 * rows * packed * width,
        )
        arrived = to_owners(outgoing)
        route_args = (
            gsel,
            *[c[1] for c in cands],
            *[c[2] for c in cands],
            *[c[4] for c in cands],
            *[c[5] for c in cands],
            router_t,
            router_sum,
        )
        wide_f = sds((rows, width), F32)
        grad_normed, router_sum = run(
            functools.partial(route_bwd_kernel, tick, slots, count, micros),
            (sec, *route_args),
            [whole(a) for a in route_args],
            [wide_f, router_sum],
            [whole(wide_f), whole(router_sum)],
            cost=2 * rows * packed * width,
        )
        act = sds((packed, ffe), F32)
        stores = [
            sds((micros + 1, ffe, packed), BF),
            sds((micros + 1, width, packed), BF),
            sds((micros + 1, packed, ffe), BF),
            sds((micros + 1, packed, ffe), BF),
            sds((micros + 1, packed, width), BF),
        ]
        anywhere = pl.BlockSpec(memory_space=pl.ANY)
        old = [] if store is None else list(store[:2])
        a1, a2, hidden_t, packed_t = run(
            functools.partial(again_kernel, tick, count),
            (sec, *[c[0] for c in cands], gate_w, up_w, *old),
            [whole(buf_full)] * count + [in_block, in_block] + [anywhere] * len(old),
            [act, act, *stores[:2]],
            [
                act_block,
                act_block,
                slot_block((tile, packed), lambda i: (i, 0)),
                slot_block((width, packed), lambda i: (0, 0)),
            ],
            grid=(steps,),
            aliases={3 + count + i: 2 + i for i in range(len(old))},
            cost=2 * matmul,
        )
        old = [] if store is None else list(store[2:])
        args = [arrived, down_w, a1, a2] + ([] if last else [gate_w, up_w])
        specs = [whole(buf_full), down_block, act_block, act_block]
        specs += [] if last else [in_block, in_block]
        outs = stores[2:] + ([] if last else [buf_full])
        out_specs = [
            slot_block((packed, tile), lambda i: (0, i)),
            slot_block((packed, tile), lambda i: (0, i)),
            slot_block((packed, width), lambda i: (0, 0)),
        ] + ([] if last else [whole(buf_full)])
        got = run(
            functools.partial(expert_bwd_kernel, last),
            (sec, *args, *old),
            specs + [anywhere] * len(old),
            outs,
            out_specs,
            grid=(steps,),
            scratch=[] if last else [pltpu.VMEM((packed, width), F32)],
            aliases={1 + len(args) + i: i for i in range(len(old))},
            cost=matmul if last else 3 * matmul,
        )
        store = (hidden_t, packed_t, *got[:3])
        if last:
            break
        returned = to_owners(got[3])
        [grad_in] = run(
            functools.partial(combine_bwd_kernel, tick, count),
            (sec, returned, places, grad_normed, gsel, *[c[2] for c in cands]),
            [buf_block, place_block(micro_of), whole(wide_f), whole(row_full)]
            + [whole(row_full)] * count,
            [row_full],
            [whole(row_full)],
            grid=(col_steps,),
            scratch=[pltpu.VMEM((rows, width), F32)],
            cost=2 * rows * packed * width,
        )
        incoming = from_behind(grad_in, "section", -1)

    router_parts = lax.all_gather(router_sum.astype(BF), plane, axis=0, tiled=False)
    router_out = jnp.sum(router_parts.astype(F32), axis=0).T[None]

    hidden_t, packed_t, gate_rows, up_rows, out_rows = store
    act_pair = pl.BlockSpec((micros, packed, ffe), lambda i, s: (0, 0, 0))
    grad_gate, grad_up, grad_down = run(
        weights_kernel,
        (sec, packed_t, gate_rows, up_rows, hidden_t, out_rows),
        [
            pl.BlockSpec((micros, chunk, packed), lambda i, s: (0, i, 0)),
            act_pair,
            act_pair,
            pl.BlockSpec((micros, ffe, packed), lambda i, s: (0, 0, 0)),
            pl.BlockSpec((micros, packed, chunk), lambda i, s: (0, 0, i)),
        ],
        [sds((width, ffe), BF), sds((width, ffe), BF), sds((ffe, width), BF)],
        [
            pl.BlockSpec((chunk, ffe), lambda i, s: (i, 0)),
            pl.BlockSpec((chunk, ffe), lambda i, s: (i, 0)),
            pl.BlockSpec((ffe, chunk), lambda i, s: (0, i)),
        ],
        grid=(col_steps,),
        cost=6 * matmul,
    )
    return (
        mean_loss,
        head_total,
        router_out,
        grad_gate[None, None],
        grad_up[None, None],
        grad_down[None, None],
    )


def solution(mesh):
    experts = P("section", plane, None, None)
    return jax.shard_map(
        shards,
        mesh=mesh,
        in_specs=(
            P(None, plane, None),
            P("section", None, plane, None),
            P(None, plane),
            P("section", None, None),
            P(),
            experts,
            experts,
            experts,
        ),
        out_specs=(P(), P(), P("section", None, None), experts, experts, experts),
        check_vma=False,
    )
```

```python
import functools

import jax
import jax.numpy as jnp
from jax import lax
from jax.experimental import pallas as pl
from jax.experimental.pallas import tpu as pltpu
from jax.sharding import PartitionSpec as P

soft_cap = 30.0
norm_eps = 1e-06
BF = jnp.bfloat16
F32 = jnp.float32
plane = ("expert", "dp")
MIB = 1 << 20


def dot(left, right, dims):
    return lax.dot_general(left, right, (dims, ((), ())), preferred_element_type=F32)


def nn(left, right):
    return dot(left, right, ((1,), (0,)))


def nt(left, right):
    return dot(left, right, ((1,), (1,)))


def tn(left, right):
    return dot(left, right, ((0,), (0,)))


def sds(shape, dtype):
    return jax.ShapeDtypeStruct(shape, dtype)


def whole(array):
    rank = len(array.shape)
    return pl.BlockSpec(array.shape, lambda *_: (0,) * rank)


class Far:
    def __init__(self, array):
        self.value = pltpu.with_memory_space_constraint(array, pltpu.HBM)


def far(arrays):
    return [Far(a) for a in arrays]


def far_out(shape):
    return pltpu.HBM(shape.shape, shape.dtype)


def run(kernel, args, in_specs, outs, out_specs, grid=(1,), scratch=(), aliases=None, cost=1e9, room=20):
    args = [a.value if isinstance(a, Far) else a for a in args]
    moved = sum(a.size * a.dtype.itemsize for a in args[1:])
    return pl.pallas_call(
        kernel,
        grid_spec=pltpu.PrefetchScalarGridSpec(
            num_scalar_prefetch=1,
            grid=grid,
            in_specs=in_specs,
            out_specs=out_specs,
            scratch_shapes=list(scratch),
        ),
        out_shape=outs,
        input_output_aliases=aliases or {},
        compiler_params=pltpu.CompilerParams(vmem_limit_bytes=room * MIB),
        cost_estimate=pl.CostEstimate(flops=int(cost), bytes_accessed=moved, transcendentals=0),
    )(*args)


def normalize(layer_in):
    hidden_f = layer_in.astype(F32)
    inv_rms = lax.rsqrt(jnp.mean(hidden_f * hidden_f, axis=-1, keepdims=True) + norm_eps)
    return hidden_f, inv_rms, (hidden_f * inv_rms).astype(BF)


def hi_lo(values):
    high = values.astype(BF)
    return high, (values - high.astype(F32)).astype(BF)


def spreading(experts, slots):
    shape = (experts, experts * slots)
    column = lax.broadcasted_iota(jnp.int32, shape, 1)
    row = lax.broadcasted_iota(jnp.int32, shape, 0)
    return ((column // slots) == row).astype(F32).astype(BF)


def pick(flag, refs):
    if len(refs) == 1:
        return refs[0][...]
    return jnp.where(flag, refs[0][...], refs[1][...])


def place_kernel(slots, sec, ids_ref, pt_ref):
    micros, rows, width = pt_ref.shape
    column = lax.broadcasted_iota(jnp.int32, (rows, width), 1)
    expert = column // slots
    slot = (column - expert * slots).astype(F32)
    below = (
        lax.broadcasted_iota(jnp.int32, (rows, rows), 0)
        > lax.broadcasted_iota(jnp.int32, (rows, rows), 1)
    ).astype(F32).astype(BF)
    for micro in range(micros):
        ids = ids_ref[micro]
        named = jnp.zeros((rows, width), F32)
        for k in range(ids.shape[1]):
            named = named + (ids[:, k : k + 1] == expert).astype(F32)
        before = nn(below, named.astype(BF))
        here = (named > 0.5) & (before == slot)
        pt_ref[micro] = here.astype(F32).astype(BF)


def prep_fwd_kernel(both, sec, *refs):
    ins, (pt_ref, h_ref, n_ref, out_ref) = refs[:-4], refs[-4:]
    step = pl.program_id(0)
    chunk = out_ref.shape[1]

    @pl.when(step == 0)
    def _():
        layer_in = pick(sec[0] == 0, ins)
        h_ref[...] = layer_in
        n_ref[...] = normalize(layer_in)[2]

    cols = n_ref[:, pl.ds(pl.multiple_of(step * chunk, chunk), chunk)]
    out_ref[...] = tn(pt_ref[0], cols).astype(BF)


def route_fwd_kernel(slots, sec, n_ref, router_ref, pt_ref, phl_ref, p_ref, c2_ref):
    logits = nn(n_ref[...], router_ref[...])
    spread = spreading(logits.shape[1], slots)
    high, low = hi_lo(logits)
    lowest = (logits - high.astype(F32) - low.astype(F32)).astype(BF)
    wide = nn(high, spread) + nn(low, spread) + nn(lowest, spread)
    tanh = jnp.tanh(wide / soft_cap)
    weights = pt_ref[0].astype(F32) * jnp.exp(soft_cap * tanh)
    probs = weights / jnp.sum(weights, axis=-1, keepdims=True)
    high, low = hi_lo(probs)
    rows = probs.shape[0]
    phl_ref[:rows] = high
    phl_ref[rows:] = low
    p_ref[...] = probs
    c2_ref[...] = 1.0 - tanh * tanh


def expert_fwd_kernel(first, sec, x_ref, wg_ref, wu_ref, wd_ref, *refs):
    out_ref, hidden_ref = refs[-2:]
    step = pl.program_id(0)
    tile = wg_ref.shape[1]

    @pl.when(step < first)
    def _():
        packed = x_ref[...]
        gate = nn(packed, wg_ref[...])
        up = nn(packed, wu_ref[...])
        cols = pl.ds(pl.multiple_of(step * tile, tile), tile)
        hidden_ref[:, cols] = (gate * jax.nn.sigmoid(gate) * up).astype(BF)

    @pl.when(step >= first)
    def _():
        out_ref[...] = nn(hidden_ref[...], wd_ref[...]).astype(BF)


def turn_kernel(sec, wg_ref, wu_ref, wd_ref, dep_ref, gu_ref, down_ref):
    tile = wg_ref.shape[1]
    gu_ref[:tile] = wg_ref[...].T
    gu_ref[tile:] = wu_ref[...].T
    down_ref[...] = wd_ref[...].T


def combine_fwd_kernel(sec, ret_ref, h_ref, phl_ref, out_ref):
    rows = h_ref.shape[0]
    both = nn(phl_ref[...], ret_ref[...])
    out_ref[...] = (h_ref[...].astype(F32) + (both[:rows] + both[rows:])).astype(BF)


def head_kernel(sec, final_ref, head_ref, label_ref, gtop_ref, glog_ref, loss_ref):
    class_logits = soft_cap * jnp.tanh(nn(final_ref[...], head_ref[...]) / soft_cap)
    weights = jnp.exp(class_logits)
    total = jnp.sum(weights, axis=-1, keepdims=True)
    hot = (lax.broadcasted_iota(jnp.int32, weights.shape, 1) == label_ref[...]).astype(F32)
    token_loss = jnp.log(total) - jnp.sum(hot * class_logits, axis=-1, keepdims=True)
    scaled = class_logits / soft_cap
    glog = ((weights / total - hot) * (1.0 - scaled * scaled)).astype(BF)
    glog_ref[...] = glog
    gtop_ref[...] = nt(glog, head_ref[...]).astype(BF)
    loss_ref[...] = jnp.broadcast_to(jnp.sum(token_loss, axis=0, keepdims=True), loss_ref.shape)


def head_sum_kernel(sec, *refs):
    ins, out_ref = refs[:-2], refs[-1]
    out_ref[...] = sum(
        tn(ins[i][...], ins[i + 1][...]) for i in range(0, len(ins), 2)
    ).astype(BF)


def piece_kernel(experts, sec, in_ref, out_ref):
    share = in_ref.shape[0] // experts
    total = in_ref[:share].astype(F32)
    for part in range(1, experts):
        total = total + in_ref[part * share : (part + 1) * share].astype(F32)
    high, low = hi_lo(total)
    out_ref[:share] = high
    out_ref[share:] = low


def prep_bwd_kernel(tick, n_g, n_p, sec, *refs):
    g_refs, phl_refs, (g_ref, out_ref) = refs[:n_g], refs[n_g : n_g + n_p], refs[n_g + n_p :]
    flag = sec[0] == sec[1] - tick
    step = pl.program_id(0)
    chunk = out_ref.shape[1]

    @pl.when(step == 0)
    def _():
        found = [ref[: g_ref.shape[0]] for ref in g_refs]
        g_ref[...] = found[0] if n_g == 1 else jnp.where(flag, found[0], found[1])

    cols = g_ref[:, pl.ds(pl.multiple_of(step * chunk, chunk), chunk)]
    probs = pick(flag, phl_refs)
    out_ref[...] = tn(probs, jnp.concatenate([cols, cols], axis=0)).astype(BF)


def route_bwd_kernel(tick, slots, n, micros, sec, g_ref, *refs):
    r_refs, h_refs, p_refs, c_refs = (refs[i * n : (i + 1) * n] for i in range(4))
    router_t_ref, acc_in_ref = refs[4 * n : 4 * n + 2]
    carry_refs, (gn_ref, acc_ref) = refs[4 * n + 2 : -2], refs[-2:]
    flag = sec[0] == sec[1] - tick
    micro = tick - (sec[1] - 1 - sec[0])
    active = (micro >= 0) & (micro < micros)
    grad = g_ref[...]
    grad_prob = nt(grad, pick(flag, r_refs))
    probs = pick(flag, p_refs)
    mean = jnp.sum(probs * grad_prob, axis=-1, keepdims=True)
    grad_chosen = (probs * (grad_prob - mean) * pick(flag, c_refs)).astype(BF)
    experts = router_t_ref.shape[0]
    grad_route = nt(grad_chosen, spreading(experts, slots)).astype(BF)
    gn_ref[...] = nn(grad_route, router_t_ref[...])
    normed = normalize(pick(flag, h_refs))[2]
    total = acc_in_ref[...] + jnp.where(active, tn(grad_route, normed), 0.0)
    if carry_refs:
        acc_ref[:experts] = total.astype(BF)
        acc_ref[experts:] = carried(sec, grad.shape[0], carry_refs)
    else:
        acc_ref[...] = total


def again_kernel(tick, n, sec, *refs):
    x_refs = refs[:n]
    wg_ref, wu_ref = refs[n : n + 2]
    a1_ref, a2_ref, ht_ref, xt_ref = refs[-4:]
    packed = pick(sec[0] == sec[1] - tick, x_refs)
    gate = nn(packed, wg_ref[...])
    up = nn(packed, wu_ref[...])
    sigmoid = jax.nn.sigmoid(gate)
    silu = gate * sigmoid
    a1_ref[...] = (up * sigmoid * (1.0 + gate * (1.0 - sigmoid))).astype(BF)
    a2_ref[...] = silu.astype(BF)
    ht_ref[0] = (silu * up).astype(BF).T

    @pl.when(pl.program_id(0) == 0)
    def _():
        xt_ref[0] = packed.T


def expert_bwd_kernel(first, sec, dy_ref, wd_ref, a1_ref, a2_ref, wgu_ref, *refs):
    gg_ref, gu_ref, dys_ref, out_ref, both_ref = refs[-5:]
    step = pl.program_id(0)
    tile = wd_ref.shape[1]

    @pl.when(step == 0)
    def _():
        dys_ref[0] = dy_ref[...]

    @pl.when(step < first)
    def _():
        grad_hidden = nn(dy_ref[...], wd_ref[...])
        gg = (grad_hidden * a1_ref[...].astype(F32)).astype(BF)
        gu = (grad_hidden * a2_ref[...].astype(F32)).astype(BF)
        gg_ref[0] = gg
        gu_ref[0] = gu
        at = pl.multiple_of(step * 2 * tile, tile)
        both_ref[:, pl.ds(at, tile)] = gg
        both_ref[:, pl.ds(pl.multiple_of(at + tile, tile), tile)] = gu

    @pl.when(step >= first)
    def _():
        out_ref[...] = nn(both_ref[...], wgu_ref[...]).astype(BF)


def earlier_kernel(sec, xt_ref, gg_ref, gu_ref, ht_ref, dy_ref, gate_ref, up_ref, down_ref, dy_now):
    done = sec[0] != 0

    @pl.when(pl.program_id(0) == 0)
    def _():
        dy_now[...] = jnp.where(done, dy_ref[1], jnp.zeros((), BF))

    gg = jnp.where(done, gg_ref[1], jnp.zeros((), BF))
    gu = jnp.where(done, gu_ref[1], jnp.zeros((), BF))
    gate_ref[...] = (nn(xt_ref[0], gg_ref[0]) + nn(xt_ref[1], gg)).astype(BF)
    up_ref[...] = (nn(xt_ref[0], gu_ref[0]) + nn(xt_ref[1], gu)).astype(BF)
    down_ref[...] = (nn(ht_ref[0], dy_ref[0]) + nn(ht_ref[1], dy_now[...])).astype(BF)


def final_kernel(sec, dy_ref, wd_ref, a1_ref, a2_ref, xt_ref, ht_ref, *refs):
    gate_old, up_old, down_old, gate_ref, up_ref, down_ref, dy_now = refs
    mine = sec[0] == 0

    @pl.when(pl.program_id(0) == 0)
    def _():
        dy_now[...] = jnp.where(mine, dy_ref[...], jnp.zeros((), BF))

    grad_hidden = nn(dy_now[...], wd_ref[...])
    gg = (grad_hidden * a1_ref[...].astype(F32)).astype(BF)
    gu = (grad_hidden * a2_ref[...].astype(F32)).astype(BF)
    gate_ref[...] = (gate_old[...].astype(F32) + nn(xt_ref[0], gg)).astype(BF)
    up_ref[...] = (up_old[...].astype(F32) + nn(xt_ref[0], gu)).astype(BF)
    down_ref[...] = (down_old[...].astype(F32) + nn(ht_ref[0], dy_now[...])).astype(BF)


def tail_kernel(held, sec, in_ref, router_ref, head_ref, loss_ref):
    blocks = in_ref.shape[0]
    experts = router_ref.shape[0]
    total = in_ref[0, :experts].astype(F32)
    for block in range(1, blocks):
        total = total + in_ref[block, :experts].astype(F32)
    step = pl.program_id(0)

    @pl.when(step == 0)
    def _():
        router_ref[...] = total

    @pl.when(step > 0)
    def _():
        router_ref[...] += total

    for block in range(blocks):
        rest = in_ref[block, experts:].astype(F32)
        head_ref[block] = rest[:held] + rest[held : 2 * held]
        loss_ref[block : block + 1] = rest[2 * held : 2 * held + 1, : loss_ref.shape[1]]


def carried(sec, rows, refs):
    own = refs[0][...]
    if len(refs) == 1:
        return own
    return jnp.where(sec[0] == sec[1] - 1, own, refs[1][rows:])


def combine_bwd_kernel(tick, n, sec, ret_ref, pt_ref, gn_ref, g_ref, *refs):
    h_refs, carry_refs, (out_ref, sum_ref) = refs[:n], refs[n:-2], refs[-2:]
    rows = g_ref.shape[0]
    step = pl.program_id(0)
    chunk = ret_ref.shape[1]
    cols = pl.ds(pl.multiple_of(step * chunk, chunk), chunk)
    sum_ref[:, cols] = nn(pt_ref[0], ret_ref[...])

    @pl.when(step == pl.num_programs(0) - 1)
    def _():
        hidden_f, inv_rms, _ = normalize(pick(sec[0] == sec[1] - tick, h_refs))
        grad_normed = sum_ref[...] + gn_ref[...]
        normed_f = hidden_f * inv_rms
        mean = jnp.mean(grad_normed * normed_f, axis=-1, keepdims=True)
        out_ref[:rows] = (
            g_ref[...].astype(F32) + inv_rms * (grad_normed - normed_f * mean)
        ).astype(BF)
        if carry_refs:
            out_ref[rows:] = carried(sec, rows, carry_refs)


def to_owners(rows):
    return lax.all_to_all(rows, plane, split_axis=0, concat_axis=0, tiled=True)


def from_behind(block, axis, distance):
    devices = range(lax.axis_size(axis))
    route = [(i - distance, i) for i in devices if i - distance in devices]
    return lax.ppermute(block, axis, route)


def shards(tokens, expert_ids, labels, router, class_head, w_gate, w_up, w_down):
    sections = lax.axis_size("section")
    section = lax.axis_index("section")
    experts = lax.axis_size(plane)
    micros, rows, width = tokens.shape
    top = expert_ids.shape[3]
    slots = 2 * rows * top // experts
    packed = experts * slots
    router_w = router[0]
    router_t = router_w.T
    gate_w, up_w, down_w = w_gate[0, 0], w_up[0, 0], w_down[0, 0]
    ffe = gate_w.shape[1]
    ticks = micros + sections - 1
    sec = jnp.stack([section, jnp.int32(sections)]).astype(jnp.int32)
    tile = 256
    chunk = 1024
    steps = ffe // tile
    col_steps = width // chunk
    row_block = pl.BlockSpec((rows, chunk), lambda i, s: (0, i))
    buf_block = pl.BlockSpec((packed, chunk), lambda i, s: (0, i))
    in_block = pl.BlockSpec((width, tile), lambda i, s: (0, i))
    down_block = pl.BlockSpec((tile, width), lambda i, s: (i, 0))
    act_block = pl.BlockSpec((packed, tile), lambda i, s: (0, i))
    row_full = sds((rows, width), BF)
    buf_full = sds((packed, width), BF)
    buf_out = pltpu.HBM((packed, width), BF)
    wide_chunk = 1024
    late_block = pl.BlockSpec((packed, wide_chunk), lambda i, s: (0, jnp.maximum(i - steps, 0)))
    anywhere = pl.BlockSpec(memory_space=pl.ANY)
    matmul = 2.0 * packed * width * ffe

    [places] = run(
        functools.partial(place_kernel, slots),
        (sec, expert_ids[0]),
        [whole(expert_ids[0])],
        [sds((micros, rows, packed), BF)],
        [whole(sds((micros, rows, packed), BF))],
    )

    def place_block(micro_of):
        return pl.BlockSpec(
            (1, rows, packed), lambda i, s: (jnp.clip(micro_of(s), 0, micros - 1), 0, 0)
        )

    saved = []
    finals = []
    incoming = None
    for tick in range(ticks):
        if tick == 0:
            ins = (tokens[0],)
        elif tick < micros:
            ins = (tokens[tick], incoming)
        else:
            ins = (incoming,)
        micro_spec = place_block(lambda s, tick=tick: tick - s[0])
        layer_in, normed, outgoing = run(
            functools.partial(prep_fwd_kernel, len(ins) == 2),
            (sec, *ins, places),
            [whole(row_full)] * len(ins) + [micro_spec],
            [far_out(row_full), row_full, buf_out],
            [whole(row_full), whole(row_full), buf_block],
            grid=(col_steps,),
            cost=2 * rows * packed * width,
        )
        arrived = to_owners(outgoing)
        wide = sds((rows, packed), F32)
        two = sds((2 * rows, packed), BF)
        probs_two, probs, slope = run(
            functools.partial(route_fwd_kernel, slots),
            (sec, normed, router_w, places),
            [whole(row_full), whole(router_w), micro_spec],
            [far_out(two), far_out(wide), far_out(wide)],
            [whole(two), whole(wide), whole(wide)],
            cost=2 * rows * width * experts,
        )
        if tick == 1:
            turned_gu, turned_down = run(
                turn_kernel,
                (sec, *far([gate_w, up_w, down_w, outgoing])),
                [in_block, in_block, down_block, anywhere],
                [pltpu.HBM((2 * ffe, width), BF), pltpu.HBM((width, ffe), BF)],
                [pl.BlockSpec((2 * tile, width), lambda i, s: (i, 0)), in_block],
                grid=(steps,),
                cost=matmul,
            )
            after = (turned_gu,)
        else:
            after = ()
        [results] = run(
            functools.partial(expert_fwd_kernel, steps),
            (sec, arrived, gate_w, up_w, down_w, *far(after)),
            [
                whole(buf_full),
                pl.BlockSpec((width, tile), lambda i, s: (0, jnp.minimum(i, steps - 1))),
                pl.BlockSpec((width, tile), lambda i, s: (0, jnp.minimum(i, steps - 1))),
                pl.BlockSpec((ffe, wide_chunk), lambda i, s: (0, jnp.maximum(i - steps, 0))),
                *[anywhere for _ in after],
            ],
            [buf_out],
            [late_block],
            grid=(steps + width // wide_chunk,),
            scratch=[pltpu.VMEM((packed, ffe), BF)],
            cost=3 * matmul,
            room=24,
        )
        returned = to_owners(results)
        [layer_out] = run(
            combine_fwd_kernel,
            (sec, returned, *far([layer_in, probs_two])),
            [buf_block, row_block, whole(two)],
            [row_full],
            [row_block],
            grid=(col_steps,),
            cost=4 * rows * packed * width,
        )
        saved.append((arrived, returned, layer_in, probs_two, probs, slope))
        if tick + 1 < ticks:
            incoming = from_behind(layer_out, "section", 1)
        micro = tick - (sections - 1)
        if micro >= 0:
            label_col = labels[micro][:, None]
            glog_full, loss_full = sds((rows, class_head.shape[1]), BF), sds((8, 128), F32)
            finals.append(
                (
                    layer_out,
                    *run(
                        head_kernel,
                        (sec, layer_out, class_head, label_col),
                        [whole(row_full), whole(class_head), whole(label_col)],
                        [far_out(row_full), far_out(glog_full), far_out(loss_full)],
                        [whole(row_full), whole(glog_full), whole(loss_full)],
                        cost=4 * rows * width * class_head.shape[1],
                    ),
                )
            )

    share = width // experts
    carry_rows = 16
    classes = class_head.shape[1]
    router_sum = jnp.zeros((experts, width), F32)
    store = None
    for tick in range(ticks):
        at = [
            s_num + tick - (sections - 1 - s_num)
            for s_num in reversed(range(sections))
            if 0 <= tick - (sections - 1 - s_num) < micros
        ]
        cands = [saved[t] for t in at]
        if tick == 0:
            grads = (finals[0][1],)
        elif tick < micros:
            grads = (finals[tick][1], incoming)
        else:
            grads = (incoming,)
        micro_of = lambda s, tick=tick: tick - (s[1] - 1 - s[0])
        last = tick + 1 == ticks

        def slot_block(shape, place, micro_of=micro_of):
            def index(i, s):
                micro = micro_of(s)
                return (jnp.where((micro >= 0) & (micro < micros), micro, micros), *place(i))

            return pl.BlockSpec((1, *shape), index)

        count = len(cands)
        gsel, outgoing = run(
            functools.partial(prep_bwd_kernel, tick, len(grads), count),
            (sec, *grads, *far([c[3] for c in cands])),
            [whole(a) for a in grads] + [whole(c[3]) for c in cands],
            [far_out(row_full), buf_out],
            [whole(row_full), buf_block],
            grid=(col_steps,),
            cost=4 * rows * packed * width,
        )
        arrived = to_owners(outgoing)
        route_args = (
            gsel,
            *[c[1] for c in cands],
            *[c[2] for c in cands],
            *[c[4] for c in cands],
            *[c[5] for c in cands],
            router_t,
            router_sum,
        )
        wide_f = sds((rows, width), F32)
        acc_full = sds((experts, width), F32)
        if last:
            route_args = (*route_args, own, incoming)
            acc_full = sds((experts + carry_rows, width), BF)
        grad_normed, router_sum = run(
            functools.partial(route_bwd_kernel, tick, slots, count, micros),
            (sec, *far(route_args)),
            [whole(a) for a in route_args],
            [far_out(wide_f), far_out(acc_full)],
            [whole(wide_f), whole(acc_full)],
            cost=2 * rows * packed * width,
        )
        act = sds((packed, ffe), BF)
        stores = [
            sds((micros + 1, ffe, packed), BF),
            sds((micros + 1, width, packed), BF),
            sds((micros + 1, packed, ffe), BF),
            sds((micros + 1, packed, ffe), BF),
            sds((micros + 1, packed, width), BF),
        ]
        old = [] if store is None else list(store[:2])
        a1, a2, hidden_t, packed_t = run(
            functools.partial(again_kernel, tick, count),
            (sec, *far([c[0] for c in cands]), *far([gate_w, up_w]), *far(old)),
            [whole(buf_full)] * count + [in_block, in_block] + [anywhere] * len(old),
            [far_out(act), far_out(act), *[far_out(a) for a in stores[:2]]],
            [
                act_block,
                act_block,
                slot_block((tile, packed), lambda i: (i, 0)),
                slot_block((width, packed), lambda i: (0, 0)),
            ],
            grid=(steps,),
            aliases={3 + count + i: 2 + i for i in range(len(old))},
            cost=2 * matmul,
            room=28,
        )
        if tick == 1:
            head_full = sds((width, classes), BF)
            head_args = [part for final in finals for part in (final[0], final[2])]
            [head_term] = run(
                head_sum_kernel,
                (sec, *far(head_args), *far([a1])),
                [*[whole(a) for a in head_args], anywhere],
                [far_out(head_full)],
                [whole(head_full)],
                cost=4 * rows * width * classes,
            )
            pieces = to_owners(head_term)
            piece_full = sds((2 * share, classes), BF)
            [piece] = run(
                functools.partial(piece_kernel, experts),
                (sec, pieces),
                [whole(pieces)],
                [piece_full],
                [whole(piece_full)],
            )
            loss_pair = jnp.stack(hi_lo(sum(final[3][0, 0] for final in finals)))
            flat = jnp.concatenate([piece.reshape(-1), loss_pair])
            own = jnp.pad(flat, (0, carry_rows * width - flat.size)).reshape(carry_rows, width)
        if last:
            break
        old = [] if store is None else list(store[2:])
        args = [arrived, turned_down, a1, a2, turned_gu]
        early = lambda i: jnp.minimum(i, steps - 1)
        got = run(
            functools.partial(expert_bwd_kernel, steps),
            (sec, arrived, *far([turned_down, a1, a2, turned_gu, *old])),
            [
                whole(buf_full),
                pl.BlockSpec((width, tile), lambda i, s: (0, early(i))),
                pl.BlockSpec((packed, tile), lambda i, s: (0, early(i))),
                pl.BlockSpec((packed, tile), lambda i, s: (0, early(i))),
                pl.BlockSpec(
                    (2 * ffe, wide_chunk), lambda i, s: (0, jnp.maximum(i - steps, 0))
                ),
                *[anywhere] * len(old),
            ],
            [*[far_out(a) for a in stores[2:]], buf_out],
            [
                slot_block((packed, tile), lambda i: (0, early(i))),
                slot_block((packed, tile), lambda i: (0, early(i))),
                slot_block((packed, width), lambda i: (0, 0)),
                late_block,
            ],
            grid=(steps + width // wide_chunk,),
            scratch=[pltpu.VMEM((packed, 2 * ffe), BF)],
            room=32,
            aliases={1 + len(args) + i: i for i in range(len(old))},
            cost=3 * matmul,
        )
        store = (hidden_t, packed_t, *got[:3])
        returned = to_owners(got[3])
        carry = [] if tick == 0 else [own] if tick == 1 else [own, incoming]
        grad_full = sds((rows + (carry_rows if carry else 0), width), BF)
        [grad_in] = run(
            functools.partial(combine_bwd_kernel, tick, count),
            (sec, returned, places, *far([grad_normed, gsel, *[c[2] for c in cands]]), *carry),
            [buf_block, place_block(micro_of), whole(wide_f), whole(row_full)]
            + [whole(row_full)] * count
            + [whole(a) for a in carry],
            [grad_full],
            [whole(grad_full)],
            grid=(col_steps,),
            scratch=[pltpu.VMEM((rows, width), F32)],
            cost=2 * rows * packed * width,
        )
        incoming = from_behind(grad_in, "section", -1)

    everyone = lax.all_gather(router_sum, plane, axis=0, tiled=False)
    held = share * classes // width
    router_full, head_full = sds((experts, width), F32), sds((experts, held, width), F32)
    loss_full = sds((experts, 128), F32)
    router_rows, head_rows, loss_rows = run(
        functools.partial(tail_kernel, held),
        (sec, everyone),
        [pl.BlockSpec((8, *everyone.shape[1:]), lambda i, s: (i, 0, 0))],
        [router_full, head_full, loss_full],
        [
            whole(router_full),
            pl.BlockSpec((8, held, width), lambda i, s: (i, 0, 0)),
            pl.BlockSpec((8, 128), lambda i, s: (i, 0)),
        ],
        grid=(experts // 8,),
    )
    router_out = router_rows.T[None]
    head_total = head_rows.reshape(width, classes)
    mean_loss = jnp.sum(loss_rows[:, :2]) / (micros * rows * experts)

    both_slots = lambda shape, place: pl.BlockSpec((micros, *shape), lambda i, s: (0, *place(i)))
    next_slot = lambda shape, place: pl.BlockSpec((1, *shape), lambda i, s: (1, *place(i)))
    up_tile = lambda i: (i, 0)
    side_tile = lambda i: (0, i)
    stay = lambda i: (0, 0)
    grad_shapes = [sds((width, ffe), BF), sds((width, ffe), BF), sds((ffe, width), BF)]
    earlier = run(
        earlier_kernel,
        (sec, *far([packed_t, store[2], store[3], hidden_t, store[4]])),
        [
            both_slots((width, packed), stay),
            both_slots((packed, tile), side_tile),
            both_slots((packed, tile), side_tile),
            both_slots((tile, packed), up_tile),
            both_slots((packed, width), stay),
        ],
        [far_out(a) for a in grad_shapes],
        [in_block, in_block, down_block],
        grid=(steps,),
        scratch=[pltpu.VMEM((packed, width), BF)],
        cost=6 * matmul,
        room=32,
    )
    grad_gate, grad_up, grad_down = run(
        final_kernel,
        (
            sec,
            arrived,
            *far([turned_down, a1, a2, packed_t, hidden_t, *earlier]),
        ),
        [
            whole(buf_full),
            in_block,
            act_block,
            act_block,
            next_slot((width, packed), stay),
            next_slot((tile, packed), up_tile),
            in_block,
            in_block,
            down_block,
        ],
        grad_shapes,
        [in_block, in_block, down_block],
        grid=(steps,),
        scratch=[pltpu.VMEM((packed, width), BF)],
        cost=4 * matmul,
        room=32,
    )
    return (
        mean_loss,
        head_total,
        router_out,
        grad_gate[None, None],
        grad_up[None, None],
        grad_down[None, None],
    )


def solution(mesh):
    experts = P("section", plane, None, None)
    return jax.shard_map(
        shards,
        mesh=mesh,
        in_specs=(
            P(None, plane, None),
            P("section", None, plane, None),
            P(None, plane),
            P("section", None, None),
            P(),
            experts,
            experts,
            experts,
        ),
        out_specs=(P(), P(), P("section", None, None), experts, experts, experts),
        check_vma=False,
    )
```

```python
import functools

import jax
import jax.numpy as jnp
from jax import lax
from jax.experimental import pallas as pl
from jax.experimental.pallas import tpu as pltpu
from jax.sharding import PartitionSpec as P

soft_cap = 30.0
norm_eps = 1e-06
BF = jnp.bfloat16
F32 = jnp.float32
plane = ("expert", "dp")
MIB = 1 << 20


def dot(left, right, dims):
    return lax.dot_general(left, right, (dims, ((), ())), preferred_element_type=F32)


def nn(left, right):
    return dot(left, right, ((1,), (0,)))


def nt(left, right):
    return dot(left, right, ((1,), (1,)))


def tn(left, right):
    return dot(left, right, ((0,), (0,)))


def sds(shape, dtype):
    return jax.ShapeDtypeStruct(shape, dtype)


def whole(array):
    rank = len(array.shape)
    return pl.BlockSpec(array.shape, lambda *_: (0,) * rank)


class Far:
    def __init__(self, array):
        self.value = pltpu.with_memory_space_constraint(array, pltpu.HBM)


def far(arrays):
    return [Far(a) for a in arrays]


def far_out(shape):
    return pltpu.HBM(shape.shape, shape.dtype)


def run(kernel, args, in_specs, outs, out_specs, grid=(1,), scratch=(), aliases=None, cost=1e9, room=20):
    args = [a.value if isinstance(a, Far) else a for a in args]
    moved = sum(a.size * a.dtype.itemsize for a in args[1:])
    return pl.pallas_call(
        kernel,
        grid_spec=pltpu.PrefetchScalarGridSpec(
            num_scalar_prefetch=1,
            grid=grid,
            in_specs=in_specs,
            out_specs=out_specs,
            scratch_shapes=list(scratch),
        ),
        out_shape=outs,
        input_output_aliases=aliases or {},
        compiler_params=pltpu.CompilerParams(vmem_limit_bytes=room * MIB),
        cost_estimate=pl.CostEstimate(flops=int(cost), bytes_accessed=moved, transcendentals=0),
    )(*args)


def normalize(layer_in):
    hidden_f = layer_in.astype(F32)
    inv_rms = lax.rsqrt(jnp.mean(hidden_f * hidden_f, axis=-1, keepdims=True) + norm_eps)
    return hidden_f, inv_rms, (hidden_f * inv_rms).astype(BF)


def hi_lo(values):
    high = values.astype(BF)
    return high, (values - high.astype(F32)).astype(BF)


def spreading(experts, slots):
    shape = (experts, experts * slots)
    column = lax.broadcasted_iota(jnp.int32, shape, 1)
    row = lax.broadcasted_iota(jnp.int32, shape, 0)
    return ((column // slots) == row).astype(F32).astype(BF)


def pick(flag, refs):
    if len(refs) == 1:
        return refs[0][...]
    return jnp.where(flag, refs[0][...], refs[1][...])


def place_kernel(slots, sec, ids_ref, pt_ref):
    micros, rows, width = pt_ref.shape
    column = lax.broadcasted_iota(jnp.int32, (rows, width), 1)
    expert = column // slots
    slot = (column - expert * slots).astype(F32)
    below = (
        lax.broadcasted_iota(jnp.int32, (rows, rows), 0)
        > lax.broadcasted_iota(jnp.int32, (rows, rows), 1)
    ).astype(F32).astype(BF)
    for micro in range(micros):
        ids = ids_ref[micro]
        named = jnp.zeros((rows, width), F32)
        for k in range(ids.shape[1]):
            named = named + (ids[:, k : k + 1] == expert).astype(F32)
        before = nn(below, named.astype(BF))
        here = (named > 0.5) & (before == slot)
        pt_ref[micro] = here.astype(F32).astype(BF)


def prep_fwd_kernel(both, sec, *refs):
    ins, (pt_ref, h_ref, n_ref, out_ref) = refs[:-4], refs[-4:]
    step = pl.program_id(0)
    chunk = out_ref.shape[1]

    @pl.when(step == 0)
    def _():
        layer_in = pick(sec[0] == 0, ins)
        h_ref[...] = layer_in
        n_ref[...] = normalize(layer_in)[2]

    cols = n_ref[:, pl.ds(pl.multiple_of(step * chunk, chunk), chunk)]
    out_ref[...] = tn(pt_ref[0], cols).astype(BF)


def route_fwd_kernel(slots, sec, n_ref, router_ref, pt_ref, phl_ref, p_ref, c2_ref):
    logits = nn(n_ref[...], router_ref[...])
    spread = spreading(logits.shape[1], slots)
    high, low = hi_lo(logits)
    lowest = (logits - high.astype(F32) - low.astype(F32)).astype(BF)
    wide = nn(high, spread) + nn(low, spread) + nn(lowest, spread)
    tanh = jnp.tanh(wide / soft_cap)
    weights = pt_ref[0].astype(F32) * jnp.exp(soft_cap * tanh)
    probs = weights / jnp.sum(weights, axis=-1, keepdims=True)
    high, low = hi_lo(probs)
    rows = probs.shape[0]
    phl_ref[:rows] = high
    phl_ref[rows:] = low
    p_ref[...] = probs
    c2_ref[...] = 1.0 - tanh * tanh


def expert_fwd_kernel(first, sec, x_ref, wg_ref, wu_ref, wd_ref, *refs):
    out_ref, hidden_ref = refs[-2:]
    step = pl.program_id(0)
    tile = wg_ref.shape[1]

    @pl.when(step < first)
    def _():
        packed = x_ref[...]
        gate = nn(packed, wg_ref[...])
        up = nn(packed, wu_ref[...])
        cols = pl.ds(pl.multiple_of(step * tile, tile), tile)
        hidden_ref[:, cols] = (gate * jax.nn.sigmoid(gate) * up).astype(BF)

    @pl.when(step >= first)
    def _():
        out_ref[...] = nn(hidden_ref[...], wd_ref[...]).astype(BF)


def turn_kernel(sec, wg_ref, wu_ref, wd_ref, dep_ref, gu_ref, down_ref):
    tile = wg_ref.shape[1]
    blocks, _, chunk = gu_ref.shape
    for block in range(blocks):
        gu_ref[block, :tile] = wg_ref[block * chunk : (block + 1) * chunk].T
        gu_ref[block, tile:] = wu_ref[block * chunk : (block + 1) * chunk].T
    down_ref[0] = wd_ref[...].T


def combine_fwd_kernel(sec, ret_ref, h_ref, phl_ref, *refs):
    out_ref = refs[-1]
    rows = h_ref.shape[0]
    both = nn(phl_ref[...], ret_ref[...])
    out_ref[...] = (h_ref[...].astype(F32) + (both[:rows] + both[rows:])).astype(BF)


def head_kernel(sec, final_ref, head_ref, label_ref, gtop_ref, glog_ref, loss_ref):
    class_logits = soft_cap * jnp.tanh(nn(final_ref[...], head_ref[...]) / soft_cap)
    weights = jnp.exp(class_logits)
    total = jnp.sum(weights, axis=-1, keepdims=True)
    hot = (lax.broadcasted_iota(jnp.int32, weights.shape, 1) == label_ref[...]).astype(F32)
    token_loss = jnp.log(total) - jnp.sum(hot * class_logits, axis=-1, keepdims=True)
    scaled = class_logits / soft_cap
    glog = ((weights / total - hot) * (1.0 - scaled * scaled)).astype(BF)
    glog_ref[...] = glog
    gtop_ref[...] = nt(glog, head_ref[...]).astype(BF)
    loss_ref[...] = jnp.broadcast_to(jnp.sum(token_loss, axis=0, keepdims=True), loss_ref.shape)


def head_sum_kernel(sec, *refs):
    ins, out_ref = refs[:-2], refs[-1]
    out_ref[...] = sum(
        tn(ins[i][...], ins[i + 1][...]) for i in range(0, len(ins), 2)
    ).astype(BF)


def piece_kernel(experts, sec, in_ref, out_ref):
    share = in_ref.shape[0] // experts
    total = in_ref[:share].astype(F32)
    for part in range(1, experts):
        total = total + in_ref[part * share : (part + 1) * share].astype(F32)
    high, low = hi_lo(total)
    out_ref[:share] = high
    out_ref[share:] = low


def prep_bwd_kernel(tick, n_g, n_p, sec, *refs):
    g_refs, phl_refs, (g_ref, out_ref) = refs[:n_g], refs[n_g : n_g + n_p], refs[n_g + n_p :]
    flag = sec[0] == sec[1] - tick
    step = pl.program_id(0)
    chunk = out_ref.shape[1]

    @pl.when(step == 0)
    def _():
        found = [ref[: g_ref.shape[0]] for ref in g_refs]
        g_ref[...] = found[0] if n_g == 1 else jnp.where(flag, found[0], found[1])

    cols = g_ref[:, pl.ds(pl.multiple_of(step * chunk, chunk), chunk)]
    probs = pick(flag, phl_refs)
    out_ref[...] = tn(probs, jnp.concatenate([cols, cols], axis=0)).astype(BF)


def route_bwd_kernel(tick, slots, n, micros, sec, g_ref, *refs):
    r_refs, h_refs, p_refs, c_refs = (refs[i * n : (i + 1) * n] for i in range(4))
    router_t_ref, acc_in_ref = refs[4 * n : 4 * n + 2]
    gn_ref, acc_ref = refs[-2:]
    flag = sec[0] == sec[1] - tick
    micro = tick - (sec[1] - 1 - sec[0])
    active = (micro >= 0) & (micro < micros)
    grad = g_ref[...]
    grad_prob = nt(grad, pick(flag, r_refs))
    probs = pick(flag, p_refs)
    mean = jnp.sum(probs * grad_prob, axis=-1, keepdims=True)
    grad_chosen = (probs * (grad_prob - mean) * pick(flag, c_refs)).astype(BF)
    experts = router_t_ref.shape[0]
    grad_route = nt(grad_chosen, spreading(experts, slots)).astype(BF)
    gn_ref[...] = nn(grad_route, router_t_ref[...])
    normed = normalize(pick(flag, h_refs))[2]
    total = acc_in_ref[...] + jnp.where(active, tn(grad_route, normed), 0.0)
    acc_ref[...] = total.astype(acc_ref.dtype)


def again_kernel(tick, n, sec, *refs):
    x_refs = refs[:n]
    wg_ref, wu_ref = refs[n : n + 2]
    a1_ref, a2_ref, ht_ref, xt_ref = refs[-4:]
    packed = pick(sec[0] == sec[1] - tick, x_refs)
    gate = nn(packed, wg_ref[...])
    up = nn(packed, wu_ref[...])
    sigmoid = jax.nn.sigmoid(gate)
    silu = gate * sigmoid
    a1_ref[0] = (up * sigmoid * (1.0 + gate * (1.0 - sigmoid))).astype(BF)
    a2_ref[0] = silu.astype(BF)
    ht_ref[0] = (silu * up).astype(BF).T

    @pl.when(pl.program_id(0) == 0)
    def _():
        xt_ref[0] = packed.T


def expert_bwd_kernel(first, sec, dy_ref, wd_ref, a1_ref, a2_ref, wgu_ref, *refs):
    gg_ref, gu_ref, out_ref, both_ref = refs[-4:]
    step = pl.program_id(0)
    tile = wd_ref.shape[2]

    @pl.when(step < first)
    def _():
        grad_hidden = nn(dy_ref[...], wd_ref[0])
        gg = (grad_hidden * a1_ref[0].astype(F32)).astype(BF)
        gu = (grad_hidden * a2_ref[0].astype(F32)).astype(BF)
        gg_ref[0] = gg
        gu_ref[0] = gu
        at = pl.multiple_of(step * 2 * tile, tile)
        both_ref[:, pl.ds(at, tile)] = gg
        both_ref[:, pl.ds(pl.multiple_of(at + tile, tile), tile)] = gu

    @pl.when(step >= first)
    def _():
        out_ref[...] = nn(both_ref[...], wgu_ref[0]).astype(BF)


def earlier_kernel(sec, xt_ref, gg_ref, gu_ref, ht_ref, *refs):
    arrived = refs[:-4]
    gate_ref, up_ref, down_ref, rows_ref = refs[-4:]
    done = sec[0] != 0

    @pl.when(pl.program_id(0) == 0)
    def _():
        for tick in range(len(arrived)):
            if tick > 0:

                @pl.when(sec[0] == sec[1] - tick)
                def _():
                    rows_ref[1] = arrived[tick][...]

            @pl.when(sec[0] == sec[1] - 1 - tick)
            def _():
                rows_ref[0] = arrived[tick][...]

        @pl.when(sec[0] == 0)
        def _():
            rows_ref[1] = jnp.zeros(rows_ref.shape[1:], BF)

    gg = jnp.where(done, gg_ref[1], jnp.zeros((), BF))
    gu = jnp.where(done, gu_ref[1], jnp.zeros((), BF))
    gate_ref[...] = (nn(xt_ref[0], gg_ref[0]) + nn(xt_ref[1], gg)).astype(BF)
    up_ref[...] = (nn(xt_ref[0], gu_ref[0]) + nn(xt_ref[1], gu)).astype(BF)
    down_ref[...] = (nn(ht_ref[0], rows_ref[0]) + nn(ht_ref[1], rows_ref[1])).astype(BF)


def final_kernel(first, sec, dy_ref, wd_ref, a1_ref, a2_ref, ht_ref, xt_ref, *refs):
    gate_old, up_old, down_old = refs[:3]
    gate_ref, up_ref, down_ref, dy_now, gg_all, gu_all = refs[-6:]
    mine = sec[0] == 0
    step = pl.program_id(0)
    tile = wd_ref.shape[2]

    @pl.when(step == 0)
    def _():
        dy_now[...] = jnp.where(mine, dy_ref[...], jnp.zeros((), BF))

    @pl.when(step < first)
    def _():
        grad_hidden = nn(dy_now[...], wd_ref[0])
        cols = pl.ds(pl.multiple_of(step * tile, tile), tile)
        gg_all[:, cols] = (grad_hidden * a1_ref[0].astype(F32)).astype(BF)
        gu_all[:, cols] = (grad_hidden * a2_ref[0].astype(F32)).astype(BF)
        down_ref[...] = (down_old[...].astype(F32) + nn(ht_ref[0], dy_now[...])).astype(BF)

    @pl.when(step >= first)
    def _():
        gate_ref[...] = (gate_old[...].astype(F32) + nn(xt_ref[0], gg_all[...])).astype(BF)
        up_ref[...] = (up_old[...].astype(F32) + nn(xt_ref[0], gu_all[...])).astype(BF)


def head_tail_kernel(held, sec, in_ref, head_ref, loss_ref):
    for block in range(in_ref.shape[0]):
        rest = in_ref[block].astype(F32)
        head_ref[block] = rest[:held] + rest[held : 2 * held]
        loss_ref[block : block + 1] = rest[2 * held : 2 * held + 1, : loss_ref.shape[1]]


def tail_kernel(sec, in_ref, router_ref):
    total = in_ref[0].astype(F32)
    for block in range(1, in_ref.shape[0]):
        total = total + in_ref[block].astype(F32)
    router_ref[...] = total


def combine_bwd_kernel(tick, n, sec, ret_ref, pt_ref, gn_ref, g_ref, *refs):
    h_refs, (out_ref, sum_ref) = refs[:n], refs[-2:]
    step = pl.program_id(0)
    chunk = ret_ref.shape[1]
    cols = pl.ds(pl.multiple_of(step * chunk, chunk), chunk)
    sum_ref[:, cols] = nn(pt_ref[0], ret_ref[...])

    @pl.when(step == pl.num_programs(0) - 1)
    def _():
        hidden_f, inv_rms, _ = normalize(pick(sec[0] == sec[1] - tick, h_refs))
        grad_normed = sum_ref[...] + gn_ref[...]
        normed_f = hidden_f * inv_rms
        mean = jnp.mean(grad_normed * normed_f, axis=-1, keepdims=True)
        out_ref[...] = (
            g_ref[...].astype(F32) + inv_rms * (grad_normed - normed_f * mean)
        ).astype(BF)


def to_owners(rows):
    return lax.all_to_all(rows, plane, split_axis=0, concat_axis=0, tiled=True)


def from_behind(block, axis, distance):
    devices = range(lax.axis_size(axis))
    route = [(i - distance, i) for i in devices if i - distance in devices]
    return lax.ppermute(block, axis, route)


def shards(tokens, expert_ids, labels, router, class_head, w_gate, w_up, w_down):
    sections = lax.axis_size("section")
    section = lax.axis_index("section")
    experts = lax.axis_size(plane)
    micros, rows, width = tokens.shape
    top = expert_ids.shape[3]
    slots = 2 * rows * top // experts
    packed = experts * slots
    router_w = router[0]
    router_t = router_w.T
    gate_w, up_w, down_w = w_gate[0, 0], w_up[0, 0], w_down[0, 0]
    ffe = gate_w.shape[1]
    ticks = micros + sections - 1
    sec = jnp.stack([section, jnp.int32(sections)]).astype(jnp.int32)
    tile = 256
    chunk = 1024
    steps = ffe // tile
    col_steps = width // chunk
    row_block = pl.BlockSpec((rows, chunk), lambda i, s: (0, i))
    buf_block = pl.BlockSpec((packed, chunk), lambda i, s: (0, i))
    in_block = pl.BlockSpec((width, tile), lambda i, s: (0, i))
    down_block = pl.BlockSpec((tile, width), lambda i, s: (i, 0))
    act_block = pl.BlockSpec((1, packed, tile), lambda i, s: (i, 0, 0))
    row_full = sds((rows, width), BF)
    buf_full = sds((packed, width), BF)
    buf_out = pltpu.HBM((packed, width), BF)
    wide_chunk = 1024
    chunk_b = 512
    late_block = pl.BlockSpec((packed, wide_chunk), lambda i, s: (0, jnp.maximum(i - steps, 0)))
    anywhere = pl.BlockSpec(memory_space=pl.ANY)
    matmul = 2.0 * packed * width * ffe

    [places] = run(
        functools.partial(place_kernel, slots),
        (sec, expert_ids[0]),
        [whole(expert_ids[0])],
        [sds((micros, rows, packed), BF)],
        [whole(sds((micros, rows, packed), BF))],
    )

    def place_block(micro_of):
        return pl.BlockSpec(
            (1, rows, packed), lambda i, s: (jnp.clip(micro_of(s), 0, micros - 1), 0, 0)
        )

    saved = []
    finals = []
    incoming = None
    for tick in range(ticks):
        if tick == 0:
            ins = (tokens[0],)
        elif tick < micros:
            ins = (tokens[tick], incoming)
        else:
            ins = (incoming,)
        micro_spec = place_block(lambda s, tick=tick: tick - s[0])
        layer_in, normed, outgoing = run(
            functools.partial(prep_fwd_kernel, len(ins) == 2),
            (sec, *ins, places),
            [whole(row_full)] * len(ins) + [micro_spec],
            [far_out(row_full), row_full, buf_out],
            [whole(row_full), whole(row_full), buf_block],
            grid=(col_steps,),
            cost=2 * rows * packed * width,
        )
        arrived = to_owners(outgoing)
        wide = sds((rows, packed), F32)
        two = sds((2 * rows, packed), BF)
        probs_two, probs, slope = run(
            functools.partial(route_fwd_kernel, slots),
            (sec, normed, router_w, places),
            [whole(row_full), whole(router_w), micro_spec],
            [far_out(two), far_out(wide), far_out(wide)],
            [whole(two), whole(wide), whole(wide)],
            cost=2 * rows * width * experts,
        )
        [results] = run(
            functools.partial(expert_fwd_kernel, steps),
            (sec, arrived, gate_w, up_w, down_w),
            [
                whole(buf_full),
                pl.BlockSpec((width, tile), lambda i, s: (0, jnp.minimum(i, steps - 1))),
                pl.BlockSpec((width, tile), lambda i, s: (0, jnp.minimum(i, steps - 1))),
                pl.BlockSpec((ffe, wide_chunk), lambda i, s: (0, jnp.maximum(i - steps, 0))),
            ],
            [buf_out],
            [late_block],
            grid=(steps + width // wide_chunk,),
            scratch=[pltpu.VMEM((packed, ffe), BF)],
            cost=3 * matmul,
            room=24,
        )
        returned = to_owners(results)
        after = ()
        if tick == 0:
            after = turned_gu, turned_down = run(
                turn_kernel,
                (sec, *far([gate_w, up_w, down_w, results])),
                [in_block, in_block, down_block, anywhere],
                [
                    pltpu.HBM((width // wide_chunk, 2 * ffe, wide_chunk), BF),
                    pltpu.HBM((steps, width, tile), BF),
                ],
                [
                    pl.BlockSpec((width // wide_chunk, 2 * tile, wide_chunk), lambda i, s: (0, i, 0)),
                    pl.BlockSpec((1, width, tile), lambda i, s: (i, 0, 0)),
                ],
                grid=(steps,),
                cost=matmul,
            )
        [layer_out] = run(
            combine_fwd_kernel,
            (sec, returned, *far([layer_in, probs_two, *after])),
            [buf_block, row_block, whole(two), *[anywhere for _ in after]],
            [row_full],
            [row_block],
            grid=(col_steps,),
            cost=4 * rows * packed * width,
        )
        saved.append((arrived, returned, layer_in, probs_two, probs, slope))
        if tick + 1 < ticks:
            incoming = from_behind(layer_out, "section", 1)
        micro = tick - (sections - 1)
        if micro >= 0:
            label_col = labels[micro][:, None]
            glog_full, loss_full = sds((rows, class_head.shape[1]), BF), sds((8, 128), F32)
            finals.append(
                (
                    layer_out,
                    *run(
                        head_kernel,
                        (sec, layer_out, class_head, label_col),
                        [whole(row_full), whole(class_head), whole(label_col)],
                        [far_out(row_full), far_out(glog_full), far_out(loss_full)],
                        [whole(row_full), whole(glog_full), whole(loss_full)],
                        cost=4 * rows * width * class_head.shape[1],
                    ),
                )
            )

    share = width // experts
    carry_rows = 16
    classes = class_head.shape[1]
    router_sum = jnp.zeros((experts, width), F32)
    store = None
    arrivals = []
    for tick in range(ticks):
        at = [
            s_num + tick - (sections - 1 - s_num)
            for s_num in reversed(range(sections))
            if 0 <= tick - (sections - 1 - s_num) < micros
        ]
        cands = [saved[t] for t in at]
        if tick == 0:
            grads = (finals[0][1],)
        elif tick < micros:
            grads = (finals[tick][1], incoming)
        else:
            grads = (incoming,)
        micro_of = lambda s, tick=tick: tick - (s[1] - 1 - s[0])
        last = tick + 1 == ticks

        def slot_block(shape, place, micro_of=micro_of):
            def index(i, s):
                micro = micro_of(s)
                return (jnp.where((micro >= 0) & (micro < micros), micro, micros), *place(i))

            return pl.BlockSpec((1, *shape), index)

        count = len(cands)
        gsel, outgoing = run(
            functools.partial(prep_bwd_kernel, tick, len(grads), count),
            (sec, *grads, *far([c[3] for c in cands])),
            [whole(a) for a in grads] + [whole(c[3]) for c in cands],
            [far_out(row_full), buf_out],
            [whole(row_full), buf_block],
            grid=(col_steps,),
            cost=4 * rows * packed * width,
        )
        arrived = to_owners(outgoing)
        route_args = (
            gsel,
            *[c[1] for c in cands],
            *[c[2] for c in cands],
            *[c[4] for c in cands],
            *[c[5] for c in cands],
            router_t,
            router_sum,
        )
        wide_f = sds((rows, width), F32)
        acc_full = sds((experts, width), F32)
        if last:
            acc_full = sds((experts, width), BF)
        grad_normed, router_sum = run(
            functools.partial(route_bwd_kernel, tick, slots, count, micros),
            (sec, *far(route_args)),
            [whole(a) for a in route_args],
            [far_out(wide_f), far_out(acc_full)],
            [whole(wide_f), whole(acc_full)],
            cost=2 * rows * packed * width,
        )
        act = sds((steps, packed, tile), BF)
        stores = [
            sds((micros + 1, ffe, packed), BF),
            sds((micros + 1, width, packed), BF),
            sds((micros + 1, packed, ffe), BF),
            sds((micros + 1, packed, ffe), BF),
        ]
        old = [] if store is None else list(store[:2])
        deps = far([carry]) if tick == 3 else far(earlier) if last else []
        a1, a2, hidden_t, packed_t = run(
            functools.partial(again_kernel, tick, count),
            (sec, *far([c[0] for c in cands]), *far([gate_w, up_w]), *far(old), *deps),
            [whole(buf_full)] * count + [in_block, in_block] + [anywhere] * len(old + deps),
            [far_out(act), far_out(act), *[far_out(a) for a in stores[:2]]],
            [
                act_block,
                act_block,
                slot_block((tile, packed), lambda i: (i, 0)),
                slot_block((width, packed), lambda i: (0, 0)),
            ],
            grid=(steps,),
            aliases={3 + count + i: 2 + i for i in range(len(old))},
            cost=2 * matmul,
            room=28,
        )
        if last:
            break
        old = [] if store is None else list(store[2:])
        args = [arrived, turned_down, a1, a2, turned_gu]
        early = lambda i: jnp.minimum(i, steps - 1)
        got = run(
            functools.partial(expert_bwd_kernel, steps),
            (sec, arrived, *far([turned_down, a1, a2, turned_gu, *old])),
            [
                whole(buf_full),
                pl.BlockSpec((1, width, tile), lambda i, s: (early(i), 0, 0)),
                pl.BlockSpec((1, packed, tile), lambda i, s: (early(i), 0, 0)),
                pl.BlockSpec((1, packed, tile), lambda i, s: (early(i), 0, 0)),
                pl.BlockSpec((1, 2 * ffe, wide_chunk), lambda i, s: (jnp.maximum(i - steps, 0), 0, 0)),
                *[anywhere] * len(old),
            ],
            [*[far_out(a) for a in stores[2:]], buf_out],
            [
                slot_block((packed, tile), lambda i: (0, early(i))),
                slot_block((packed, tile), lambda i: (0, early(i))),
                late_block,
            ],
            grid=(steps + width // wide_chunk,),
            scratch=[pltpu.VMEM((packed, 2 * ffe), BF)],
            room=32,
            aliases={1 + len(args) + i: i for i in range(len(old))},
            cost=3 * matmul,
        )
        store = (hidden_t, packed_t, *got[:2])
        returned = to_owners(got[2])
        arrivals.append(arrived)
        before = []
        if tick + 2 == ticks:
            both_slots = lambda shape, place: pl.BlockSpec((micros, *shape), lambda i, s: (0, *place(i)))
            up_tile = lambda i: (i, 0)
            side_tile = lambda i: (0, i)
            stay = lambda i: (0, 0)
            grad_shapes = [sds((width, ffe), BF), sds((width, ffe), BF), sds((ffe, width), BF)]
            earlier = run(
                earlier_kernel,
                (sec, *far([packed_t, store[2], store[3], hidden_t, *arrivals])),
                [
                    both_slots((width, packed), stay),
                    both_slots((packed, tile), side_tile),
                    both_slots((packed, tile), side_tile),
                    both_slots((tile, packed), up_tile),
                    *[whole(buf_full) for _ in arrivals],
                ],
                [far_out(a) for a in grad_shapes],
                [in_block, in_block, down_block],
                grid=(steps,),
                scratch=[pltpu.VMEM((micros, packed, width), BF)],
                cost=6 * matmul,
                room=44,
            )
            before = earlier
        [grad_in] = run(
            functools.partial(combine_bwd_kernel, tick, count),
            (sec, returned, places, *far([grad_normed, gsel, *[c[2] for c in cands], *before])),
            [buf_block, place_block(micro_of), whole(wide_f), whole(row_full)]
            + [whole(row_full)] * count
            + [anywhere] * len(before),
            [row_full],
            [whole(row_full)],
            grid=(col_steps,),
            scratch=[pltpu.VMEM((rows, width), F32)],
            cost=2 * rows * packed * width,
        )
        if tick == 2:
            head_full = sds((width, classes), BF)
            head_args = [part for final in finals for part in (final[0], final[2])]
            [head_term] = run(
                head_sum_kernel,
                (sec, *far(head_args), *far([grad_normed])),
                [*[whole(a) for a in head_args], anywhere],
                [far_out(head_full)],
                [whole(head_full)],
                cost=4 * rows * width * classes,
            )
            head_term, _ = lax.optimization_barrier((head_term, grad_in))
            pieces = to_owners(head_term)
            piece_full = sds((2 * share, classes), BF)
            [piece] = run(
                functools.partial(piece_kernel, experts),
                (sec, pieces),
                [whole(pieces)],
                [piece_full],
                [whole(piece_full)],
            )
            loss_pair = jnp.stack(hi_lo(sum(final[3][0, 0] for final in finals)))
            flat = jnp.concatenate([piece.reshape(-1), loss_pair])
            own = jnp.pad(flat, (0, carry_rows * width - flat.size)).reshape(carry_rows, width)
            others = [lax.ppermute(own, "section", [(sections - 1, t)]) for t in range(sections - 1)]
            carry = jnp.where(section == sections - 1, own, sum(others))
            carry_all = lax.all_gather(carry, plane, axis=0, tiled=False)
        incoming = from_behind(grad_in, "section", -1)

    everyone = lax.all_gather(router_sum, plane, axis=0, tiled=False)
    held = share * classes // width
    router_full, head_full = sds((experts, width), F32), sds((experts, held, width), F32)
    loss_full = sds((experts, 128), F32)
    head_rows, loss_rows = run(
        functools.partial(head_tail_kernel, held),
        (sec, *far([carry_all])),
        [pl.BlockSpec((8, *carry_all.shape[1:]), lambda i, s: (i, 0, 0))],
        [head_full, loss_full],
        [
            pl.BlockSpec((8, held, width), lambda i, s: (i, 0, 0)),
            pl.BlockSpec((8, 128), lambda i, s: (i, 0)),
        ],
        grid=(experts // 8,),
    )
    head_total = head_rows.reshape(width, classes)
    mean_loss = jnp.sum(loss_rows[:, :2]) / (micros * rows * experts)
    [router_rows] = run(
        tail_kernel,
        (sec, *far([everyone])),
        [pl.BlockSpec((*everyone.shape[:2], chunk_b), lambda i, s: (0, 0, i))],
        [router_full],
        [pl.BlockSpec((experts, chunk_b), lambda i, s: (0, i))],
        grid=(width // chunk_b,),
    )
    router_out = router_rows.T[None]

    next_slot = lambda shape, place: pl.BlockSpec((1, *shape), lambda i, s: (1, *place(i)))
    early = lambda i: jnp.minimum(i, steps - 1)
    late = lambda i: jnp.maximum(i - steps, 0)
    down_early = pl.BlockSpec((tile, width), lambda i, s: (early(i), 0))
    act_early = pl.BlockSpec((1, packed, tile), lambda i, s: (early(i), 0, 0))
    in_late = pl.BlockSpec((chunk_b, ffe), lambda i, s: (late(i), 0))
    grad_gate, grad_up, grad_down = run(
        functools.partial(final_kernel, steps),
        (
            sec,
            arrived,
            *far([turned_down, a1, a2, hidden_t, packed_t, *earlier, head_total]),
        ),
        [
            whole(buf_full),
            pl.BlockSpec((1, width, tile), lambda i, s: (early(i), 0, 0)),
            act_early,
            act_early,
            next_slot((tile, packed), lambda i: (early(i), 0)),
            next_slot((chunk_b, packed), lambda i: (late(i), 0)),
            in_late,
            in_late,
            down_early,
            anywhere,
        ],
        grad_shapes,
        [in_late, in_late, down_early],
        grid=(steps + width // chunk_b,),
        scratch=[
            pltpu.VMEM((packed, width), BF),
            pltpu.VMEM((packed, ffe), BF),
            pltpu.VMEM((packed, ffe), BF),
        ],
        cost=4 * matmul,
        room=32,
    )
    return (
        mean_loss,
        head_total,
        router_out,
        grad_gate[None, None],
        grad_up[None, None],
        grad_down[None, None],
    )


def solution(mesh):
    experts = P("section", plane, None, None)
    return jax.shard_map(
        shards,
        mesh=mesh,
        in_specs=(
            P(None, plane, None),
            P("section", None, plane, None),
            P(None, plane),
            P("section", None, None),
            P(),
            experts,
            experts,
            experts,
        ),
        out_specs=(P(), P(), P("section", None, None), experts, experts, experts),
        check_vma=False,
    )
```

```python
import functools

import jax
import jax.numpy as jnp
from jax import lax
from jax.experimental import pallas as pl
from jax.experimental.pallas import tpu as pltpu
from jax.sharding import PartitionSpec as P

soft_cap = 30.0
norm_eps = 1e-06
BF = jnp.bfloat16
F32 = jnp.float32
plane = ("expert", "dp")
MIB = 1 << 20


def dot(left, right, dims):
    return lax.dot_general(left, right, (dims, ((), ())), preferred_element_type=F32)


def nn(left, right):
    return dot(left, right, ((1,), (0,)))


def nt(left, right):
    return dot(left, right, ((1,), (1,)))


def tn(left, right):
    return dot(left, right, ((0,), (0,)))


def sds(shape, dtype):
    return jax.ShapeDtypeStruct(shape, dtype)


def whole(array):
    rank = len(array.shape)
    return pl.BlockSpec(array.shape, lambda *_: (0,) * rank)


class Far:
    def __init__(self, array):
        self.value = pltpu.with_memory_space_constraint(array, pltpu.HBM)


def far(arrays):
    return [Far(a) for a in arrays]


def far_out(shape):
    return pltpu.HBM(shape.shape, shape.dtype)


def run(kernel, args, in_specs, outs, out_specs, grid=(1,), scratch=(), aliases=None, cost=1e9, room=20):
    args = [a.value if isinstance(a, Far) else a for a in args]
    moved = sum(a.size * a.dtype.itemsize for a in args[1:])
    return pl.pallas_call(
        kernel,
        grid_spec=pltpu.PrefetchScalarGridSpec(
            num_scalar_prefetch=1,
            grid=grid,
            in_specs=in_specs,
            out_specs=out_specs,
            scratch_shapes=list(scratch),
        ),
        out_shape=outs,
        input_output_aliases=aliases or {},
        compiler_params=pltpu.CompilerParams(vmem_limit_bytes=room * MIB),
        cost_estimate=pl.CostEstimate(flops=int(cost), bytes_accessed=moved, transcendentals=0),
    )(*args)


def normalize(layer_in):
    hidden_f = layer_in.astype(F32)
    inv_rms = lax.rsqrt(jnp.mean(hidden_f * hidden_f, axis=-1, keepdims=True) + norm_eps)
    return hidden_f, inv_rms, (hidden_f * inv_rms).astype(BF)


def hi_lo(values):
    high = values.astype(BF)
    return high, (values - high.astype(F32)).astype(BF)


def spreading(experts, slots):
    shape = (experts, experts * slots)
    column = lax.broadcasted_iota(jnp.int32, shape, 1)
    row = lax.broadcasted_iota(jnp.int32, shape, 0)
    return ((column // slots) == row).astype(F32).astype(BF)


def pick(flag, refs):
    if len(refs) == 1:
        return refs[0][...]
    return jnp.where(flag, refs[0][...], refs[1][...])


def place_kernel(slots, sec, ids_ref, pt_ref):
    micros, rows, width = pt_ref.shape
    column = lax.broadcasted_iota(jnp.int32, (rows, width), 1)
    expert = column // slots
    slot = (column - expert * slots).astype(F32)
    below = (
        lax.broadcasted_iota(jnp.int32, (rows, rows), 0)
        > lax.broadcasted_iota(jnp.int32, (rows, rows), 1)
    ).astype(F32).astype(BF)
    for micro in range(micros):
        ids = ids_ref[micro]
        named = jnp.zeros((rows, width), F32)
        for k in range(ids.shape[1]):
            named = named + (ids[:, k : k + 1] == expert).astype(F32)
        before = nn(below, named.astype(BF))
        here = (named > 0.5) & (before == slot)
        pt_ref[micro] = here.astype(F32).astype(BF)


def prep_fwd_kernel(both, sec, *refs):
    ins, (pt_ref, h_ref, n_ref, out_ref) = refs[:-4], refs[-4:]
    step = pl.program_id(0)
    chunk = out_ref.shape[1]

    @pl.when(step == 0)
    def _():
        layer_in = pick(sec[0] == 0, ins)
        h_ref[...] = layer_in
        n_ref[...] = normalize(layer_in)[2]

    cols = n_ref[:, pl.ds(pl.multiple_of(step * chunk, chunk), chunk)]
    out_ref[...] = tn(pt_ref[0], cols).astype(BF)


def route_fwd_kernel(slots, sec, n_ref, router_ref, pt_ref, phl_ref, p_ref, c2_ref):
    logits = nn(n_ref[...], router_ref[...])
    spread = spreading(logits.shape[1], slots)
    high, low = hi_lo(logits)
    lowest = (logits - high.astype(F32) - low.astype(F32)).astype(BF)
    wide = nn(high, spread) + nn(low, spread) + nn(lowest, spread)
    tanh = jnp.tanh(wide / soft_cap)
    weights = pt_ref[0].astype(F32) * jnp.exp(soft_cap * tanh)
    probs = weights / jnp.sum(weights, axis=-1, keepdims=True)
    high, low = hi_lo(probs)
    rows = probs.shape[0]
    phl_ref[:rows] = high
    phl_ref[rows:] = low
    p_ref[...] = probs
    c2_ref[...] = 1.0 - tanh * tanh


def expert_fwd_kernel(first, sec, x_ref, wg_ref, wu_ref, wd_ref, *refs):
    out_ref, hidden_ref = refs[-2:]
    step = pl.program_id(0)
    tile = wg_ref.shape[1]

    @pl.when(step < first)
    def _():
        packed = x_ref[...]
        gate = nn(packed, wg_ref[...])
        up = nn(packed, wu_ref[...])
        cols = pl.ds(pl.multiple_of(step * tile, tile), tile)
        hidden_ref[:, cols] = (gate * jax.nn.sigmoid(gate) * up).astype(BF)

    @pl.when(step >= first)
    def _():
        out_ref[...] = nn(hidden_ref[...], wd_ref[...]).astype(BF)


def turn_kernel(sec, wg_ref, wu_ref, wd_ref, dep_ref, gu_ref, down_ref):
    tile = wg_ref.shape[1]
    blocks, _, chunk = gu_ref.shape
    for block in range(blocks):
        gu_ref[block, :tile] = wg_ref[block * chunk : (block + 1) * chunk].T
        gu_ref[block, tile:] = wu_ref[block * chunk : (block + 1) * chunk].T
    down_ref[0] = wd_ref[...].T


def combine_fwd_kernel(sec, ret_ref, h_ref, phl_ref, *refs):
    out_ref = refs[-1]
    rows = h_ref.shape[0]
    both = nn(phl_ref[...], ret_ref[...])
    out_ref[...] = (h_ref[...].astype(F32) + (both[:rows] + both[rows:])).astype(BF)


def head_kernel(sec, final_ref, head_ref, label_ref, gtop_ref, glog_ref, loss_ref):
    class_logits = soft_cap * jnp.tanh(nn(final_ref[...], head_ref[...]) / soft_cap)
    weights = jnp.exp(class_logits)
    total = jnp.sum(weights, axis=-1, keepdims=True)
    hot = (lax.broadcasted_iota(jnp.int32, weights.shape, 1) == label_ref[...]).astype(F32)
    token_loss = jnp.log(total) - jnp.sum(hot * class_logits, axis=-1, keepdims=True)
    scaled = class_logits / soft_cap
    glog = ((weights / total - hot) * (1.0 - scaled * scaled)).astype(BF)
    glog_ref[...] = glog
    gtop_ref[...] = nt(glog, head_ref[...]).astype(BF)
    loss_ref[...] = jnp.broadcast_to(jnp.sum(token_loss, axis=0, keepdims=True), loss_ref.shape)


def head_sum_kernel(sec, *refs):
    ins, out_ref = refs[:-2], refs[-1]
    out_ref[...] = sum(
        tn(ins[i][...], ins[i + 1][...]) for i in range(0, len(ins), 2)
    ).astype(BF)


def piece_kernel(experts, sec, in_ref, out_ref):
    share = in_ref.shape[0] // experts
    total = in_ref[:share].astype(F32)
    for part in range(1, experts):
        total = total + in_ref[part * share : (part + 1) * share].astype(F32)
    high, low = hi_lo(total)
    out_ref[:share] = high
    out_ref[share:] = low


def prep_bwd_kernel(tick, n_g, n_p, sec, *refs):
    g_refs, phl_refs, (g_ref, out_ref) = refs[:n_g], refs[n_g : n_g + n_p], refs[-2:]
    flag = sec[0] == sec[1] - tick
    step = pl.program_id(0)
    chunk = out_ref.shape[1]

    @pl.when(step == 0)
    def _():
        found = [ref[: g_ref.shape[0]] for ref in g_refs]
        g_ref[...] = found[0] if n_g == 1 else jnp.where(flag, found[0], found[1])

    cols = g_ref[:, pl.ds(pl.multiple_of(step * chunk, chunk), chunk)]
    probs = pick(flag, phl_refs)
    out_ref[...] = tn(probs, jnp.concatenate([cols, cols], axis=0)).astype(BF)


def route_bwd_kernel(tick, slots, n, micros, sec, g_ref, *refs):
    r_refs, h_refs, p_refs, c_refs = (refs[i * n : (i + 1) * n] for i in range(4))
    router_t_ref, acc_in_ref = refs[4 * n : 4 * n + 2]
    gn_ref, acc_ref = refs[-2:]
    flag = sec[0] == sec[1] - tick
    micro = tick - (sec[1] - 1 - sec[0])
    active = (micro >= 0) & (micro < micros)
    grad = g_ref[...]
    grad_prob = nt(grad, pick(flag, r_refs))
    probs = pick(flag, p_refs)
    mean = jnp.sum(probs * grad_prob, axis=-1, keepdims=True)
    grad_chosen = (probs * (grad_prob - mean) * pick(flag, c_refs)).astype(BF)
    experts = router_t_ref.shape[0]
    grad_route = nt(grad_chosen, spreading(experts, slots)).astype(BF)
    gn_ref[...] = nn(grad_route, router_t_ref[...])
    normed = normalize(pick(flag, h_refs))[2]
    total = acc_in_ref[...] + jnp.where(active, tn(grad_route, normed), 0.0)
    acc_ref[...] = total.astype(acc_ref.dtype)


def again_kernel(tick, n, sec, *refs):
    x_refs = refs[:n]
    wg_ref, wu_ref = refs[n : n + 2]
    a1_ref, a2_ref, ht_ref, xt_ref = refs[-4:]
    packed = pick(sec[0] == sec[1] - tick, x_refs)
    gate = nn(packed, wg_ref[...])
    up = nn(packed, wu_ref[...])
    sigmoid = jax.nn.sigmoid(gate)
    silu = gate * sigmoid
    a1_ref[0] = (up * sigmoid * (1.0 + gate * (1.0 - sigmoid))).astype(BF)
    a2_ref[0] = silu.astype(BF)
    ht_ref[0] = (silu * up).astype(BF).T

    @pl.when(pl.program_id(0) == 0)
    def _():
        xt_ref[0] = packed.T


def expert_bwd_kernel(first, sec, dy_ref, wd_ref, a1_ref, a2_ref, wgu_ref, *refs):
    gg_ref, gu_ref, out_ref, both_ref = refs[-4:]
    step = pl.program_id(0)
    tile = wd_ref.shape[2]

    @pl.when(step < first)
    def _():
        grad_hidden = nn(dy_ref[...], wd_ref[0])
        gg = (grad_hidden * a1_ref[0].astype(F32)).astype(BF)
        gu = (grad_hidden * a2_ref[0].astype(F32)).astype(BF)
        gg_ref[0] = gg
        gu_ref[0] = gu
        at = pl.multiple_of(step * 2 * tile, tile)
        both_ref[:, pl.ds(at, tile)] = gg
        both_ref[:, pl.ds(pl.multiple_of(at + tile, tile), tile)] = gu

    @pl.when(step >= first)
    def _():
        out_ref[...] = nn(both_ref[...], wgu_ref[0]).astype(BF)


def earlier_kernel(sec, xt_ref, gg_ref, gu_ref, ht_ref, *refs):
    arrived = refs[:-4]
    gate_ref, up_ref, down_ref, rows_ref = refs[-4:]
    done = sec[0] != 0

    @pl.when(pl.program_id(0) == 0)
    def _():
        for tick in range(len(arrived)):
            if tick > 0:

                @pl.when(sec[0] == sec[1] - tick)
                def _():
                    rows_ref[1] = arrived[tick][...]

            @pl.when(sec[0] == sec[1] - 1 - tick)
            def _():
                rows_ref[0] = arrived[tick][...]

        @pl.when(sec[0] == 0)
        def _():
            rows_ref[1] = jnp.zeros(rows_ref.shape[1:], BF)

    gg = jnp.where(done, gg_ref[1], jnp.zeros((), BF))
    gu = jnp.where(done, gu_ref[1], jnp.zeros((), BF))
    gate_ref[...] = (nn(xt_ref[0], gg_ref[0]) + nn(xt_ref[1], gg)).astype(BF)
    up_ref[...] = (nn(xt_ref[0], gu_ref[0]) + nn(xt_ref[1], gu)).astype(BF)
    down_ref[...] = (nn(ht_ref[0], rows_ref[0]) + nn(ht_ref[1], rows_ref[1])).astype(BF)


def final_kernel(first, sec, dy_ref, wd_ref, a1_ref, a2_ref, ht_ref, xt_ref, *refs):
    gate_old, up_old, down_old = refs[:3]
    gate_ref, up_ref, down_ref, dy_now, gg_all, gu_all = refs[-6:]
    mine = sec[0] == 0
    step = pl.program_id(0)
    tile = wd_ref.shape[2]

    @pl.when(step == 0)
    def _():
        dy_now[...] = jnp.where(mine, dy_ref[...], jnp.zeros((), BF))

    @pl.when(step < first)
    def _():
        grad_hidden = nn(dy_now[...], wd_ref[0])
        cols = pl.ds(pl.multiple_of(step * tile, tile), tile)
        gg_all[:, cols] = (grad_hidden * a1_ref[0].astype(F32)).astype(BF)
        gu_all[:, cols] = (grad_hidden * a2_ref[0].astype(F32)).astype(BF)
        down_ref[...] = (down_old[...].astype(F32) + nn(ht_ref[0], dy_now[...])).astype(BF)

    @pl.when(step >= first)
    def _():
        gate_ref[...] = (gate_old[...].astype(F32) + nn(xt_ref[0], gg_all[...])).astype(BF)
        up_ref[...] = (up_old[...].astype(F32) + nn(xt_ref[0], gu_all[...])).astype(BF)


def head_tail_kernel(held, sec, in_ref, head_ref, loss_ref):
    for block in range(in_ref.shape[0]):
        rest = in_ref[block].astype(F32)
        head_ref[block] = rest[:held] + rest[held : 2 * held]
        loss_ref[block : block + 1] = rest[2 * held : 2 * held + 1, : loss_ref.shape[1]]


def tail_kernel(sec, in_ref, router_ref):
    total = in_ref[0].astype(F32)
    for block in range(1, in_ref.shape[0]):
        total = total + in_ref[block].astype(F32)
    router_ref[...] = total


def combine_bwd_kernel(tick, n, sec, ret_ref, pt_ref, gn_ref, g_ref, *refs):
    h_refs, (out_ref, sum_ref) = refs[:n], refs[-2:]
    step = pl.program_id(0)
    chunk = ret_ref.shape[1]
    cols = pl.ds(pl.multiple_of(step * chunk, chunk), chunk)
    sum_ref[:, cols] = nn(pt_ref[0], ret_ref[...])

    @pl.when(step == pl.num_programs(0) - 1)
    def _():
        hidden_f, inv_rms, _ = normalize(pick(sec[0] == sec[1] - tick, h_refs))
        grad_normed = sum_ref[...] + gn_ref[...]
        normed_f = hidden_f * inv_rms
        mean = jnp.mean(grad_normed * normed_f, axis=-1, keepdims=True)
        out_ref[...] = (
            g_ref[...].astype(F32) + inv_rms * (grad_normed - normed_f * mean)
        ).astype(BF)


def to_owners(rows):
    return lax.all_to_all(rows, plane, split_axis=0, concat_axis=0, tiled=True)


def from_behind(block, axis, distance):
    devices = range(lax.axis_size(axis))
    route = [(i - distance, i) for i in devices if i - distance in devices]
    return lax.ppermute(block, axis, route)


def shards(tokens, expert_ids, labels, router, class_head, w_gate, w_up, w_down):
    sections = lax.axis_size("section")
    section = lax.axis_index("section")
    experts = lax.axis_size(plane)
    micros, rows, width = tokens.shape
    top = expert_ids.shape[3]
    slots = 2 * rows * top // experts
    packed = experts * slots
    router_w = router[0]
    router_t = router_w.T
    gate_w, up_w, down_w = w_gate[0, 0], w_up[0, 0], w_down[0, 0]
    ffe = gate_w.shape[1]
    ticks = micros + sections - 1
    sec = jnp.stack([section, jnp.int32(sections)]).astype(jnp.int32)
    tile = 256
    chunk = 1024
    steps = ffe // tile
    col_steps = width // chunk
    row_block = pl.BlockSpec((rows, chunk), lambda i, s: (0, i))
    buf_block = pl.BlockSpec((packed, chunk), lambda i, s: (0, i))
    in_block = pl.BlockSpec((width, tile), lambda i, s: (0, i))
    down_block = pl.BlockSpec((tile, width), lambda i, s: (i, 0))
    act_block = pl.BlockSpec((1, packed, tile), lambda i, s: (i, 0, 0))
    row_full = sds((rows, width), BF)
    buf_full = sds((packed, width), BF)
    buf_out = pltpu.HBM((packed, width), BF)
    wide_chunk = 1024
    chunk_b = 512
    late_block = pl.BlockSpec((packed, wide_chunk), lambda i, s: (0, jnp.maximum(i - steps, 0)))
    anywhere = pl.BlockSpec(memory_space=pl.ANY)
    matmul = 2.0 * packed * width * ffe

    [places] = run(
        functools.partial(place_kernel, slots),
        (sec, expert_ids[0]),
        [whole(expert_ids[0])],
        [sds((micros, rows, packed), BF)],
        [whole(sds((micros, rows, packed), BF))],
    )

    def place_block(micro_of):
        return pl.BlockSpec(
            (1, rows, packed), lambda i, s: (jnp.clip(micro_of(s), 0, micros - 1), 0, 0)
        )

    saved = []
    finals = []
    incoming = None
    for tick in range(ticks):
        if tick == 0:
            ins = (tokens[0],)
        elif tick < micros:
            ins = (tokens[tick], incoming)
        else:
            ins = (incoming,)
        micro_spec = place_block(lambda s, tick=tick: tick - s[0])
        layer_in, normed, outgoing = run(
            functools.partial(prep_fwd_kernel, len(ins) == 2),
            (sec, *ins, places),
            [whole(row_full)] * len(ins) + [micro_spec],
            [far_out(row_full), row_full, buf_out],
            [whole(row_full), whole(row_full), buf_block],
            grid=(col_steps,),
            cost=2 * rows * packed * width,
        )
        arrived = to_owners(outgoing)
        wide = sds((rows, packed), F32)
        two = sds((2 * rows, packed), BF)
        probs_two, probs, slope = run(
            functools.partial(route_fwd_kernel, slots),
            (sec, normed, router_w, places),
            [whole(row_full), whole(router_w), micro_spec],
            [far_out(two), far_out(wide), far_out(wide)],
            [whole(two), whole(wide), whole(wide)],
            cost=2 * rows * width * experts,
        )
        [results] = run(
            functools.partial(expert_fwd_kernel, steps),
            (sec, arrived, gate_w, up_w, down_w),
            [
                whole(buf_full),
                pl.BlockSpec((width, tile), lambda i, s: (0, jnp.minimum(i, steps - 1))),
                pl.BlockSpec((width, tile), lambda i, s: (0, jnp.minimum(i, steps - 1))),
                pl.BlockSpec((ffe, wide_chunk), lambda i, s: (0, jnp.maximum(i - steps, 0))),
            ],
            [buf_out],
            [late_block],
            grid=(steps + width // wide_chunk,),
            scratch=[pltpu.VMEM((packed, ffe), BF)],
            cost=3 * matmul,
            room=24,
        )
        returned = to_owners(results)
        after = ()
        if tick == 0:
            after = turned_gu, turned_down = run(
                turn_kernel,
                (sec, *far([gate_w, up_w, down_w, results])),
                [in_block, in_block, down_block, anywhere],
                [
                    pltpu.HBM((width // wide_chunk, 2 * ffe, wide_chunk), BF),
                    pltpu.HBM((steps, width, tile), BF),
                ],
                [
                    pl.BlockSpec((width // wide_chunk, 2 * tile, wide_chunk), lambda i, s: (0, i, 0)),
                    pl.BlockSpec((1, width, tile), lambda i, s: (i, 0, 0)),
                ],
                grid=(steps,),
                cost=matmul,
            )
        [layer_out] = run(
            combine_fwd_kernel,
            (sec, returned, *far([layer_in, probs_two, *after])),
            [buf_block, row_block, whole(two), *[anywhere for _ in after]],
            [row_full],
            [row_block],
            grid=(col_steps,),
            cost=4 * rows * packed * width,
        )
        saved.append((arrived, returned, layer_in, probs_two, probs, slope))
        if tick + 1 < ticks:
            incoming = from_behind(layer_out, "section", 1)
        micro = tick - (sections - 1)
        if micro >= 0:
            label_col = labels[micro][:, None]
            glog_full, loss_full = sds((rows, class_head.shape[1]), BF), sds((8, 128), F32)
            finals.append(
                (
                    layer_out,
                    *run(
                        head_kernel,
                        (sec, layer_out, class_head, label_col),
                        [whole(row_full), whole(class_head), whole(label_col)],
                        [far_out(row_full), far_out(glog_full), far_out(loss_full)],
                        [whole(row_full), whole(glog_full), whole(loss_full)],
                        cost=4 * rows * width * class_head.shape[1],
                    ),
                )
            )

    share = width // experts
    carry_rows = 16
    classes = class_head.shape[1]
    router_sum = jnp.zeros((experts, width), F32)
    store = None
    arrivals = []
    for tick in range(ticks):
        at = [
            s_num + tick - (sections - 1 - s_num)
            for s_num in reversed(range(sections))
            if 0 <= tick - (sections - 1 - s_num) < micros
        ]
        cands = [saved[t] for t in at]
        if tick == 0:
            grads = (finals[0][1],)
        elif tick < micros:
            grads = (finals[tick][1], incoming)
        else:
            grads = (incoming,)
        micro_of = lambda s, tick=tick: tick - (s[1] - 1 - s[0])
        last = tick + 1 == ticks

        def slot_block(shape, place, micro_of=micro_of):
            def index(i, s):
                micro = micro_of(s)
                return (jnp.where((micro >= 0) & (micro < micros), micro, micros), *place(i))

            return pl.BlockSpec((1, *shape), index)

        count = len(cands)
        def prep(*order):
            return run(
                functools.partial(prep_bwd_kernel, tick, len(grads), count),
                (sec, *grads, *far([*[c[3] for c in cands], *order])),
                [whole(a) for a in grads]
                + [whole(c[3]) for c in cands]
                + [anywhere] * len(order),
                [far_out(row_full), buf_out],
                [whole(row_full), buf_block],
                grid=(col_steps,),
                cost=4 * rows * packed * width,
            )

        if not last:
            gsel, outgoing = prep()
        route_args = (
            *[c[1] for c in cands],
            *[c[2] for c in cands],
            *[c[4] for c in cands],
            *[c[5] for c in cands],
            router_t,
            router_sum,
        )
        wide_f = sds((rows, width), F32)
        acc_full = sds((experts, width), F32)
        if last:
            acc_full = sds((experts, width), BF)
        grad_normed, router_sum = run(
            functools.partial(route_bwd_kernel, tick, slots, count, micros),
            (sec, grads[0] if last else Far(gsel), *far(route_args)),
            [whole(row_full)] + [whole(a) for a in route_args],
            [far_out(wide_f), far_out(acc_full)],
            [whole(wide_f), whole(acc_full)],
            cost=2 * rows * packed * width,
        )
        if last:
            _, outgoing = prep(router_sum)
        arrived = to_owners(outgoing)
        act = sds((steps, packed, tile), BF)
        stores = [
            sds((micros + 1, ffe, packed), BF),
            sds((micros + 1, width, packed), BF),
            sds((micros + 1, packed, ffe), BF),
            sds((micros + 1, packed, ffe), BF),
        ]
        old = [] if store is None else list(store[:2])
        deps = far([carry]) if tick == 3 else far(earlier) if last else []
        a1, a2, hidden_t, packed_t = run(
            functools.partial(again_kernel, tick, count),
            (sec, *far([c[0] for c in cands]), *far([gate_w, up_w]), *far(old), *deps),
            [whole(buf_full)] * count + [in_block, in_block] + [anywhere] * len(old + deps),
            [far_out(act), far_out(act), *[far_out(a) for a in stores[:2]]],
            [
                act_block,
                act_block,
                slot_block((tile, packed), lambda i: (i, 0)),
                slot_block((width, packed), lambda i: (0, 0)),
            ],
            grid=(steps,),
            aliases={3 + count + i: 2 + i for i in range(len(old))},
            cost=2 * matmul,
            room=28,
        )
        if last:
            break
        old = [] if store is None else list(store[2:])
        args = [arrived, turned_down, a1, a2, turned_gu]
        early = lambda i: jnp.minimum(i, steps - 1)
        got = run(
            functools.partial(expert_bwd_kernel, steps),
            (sec, arrived, *far([turned_down, a1, a2, turned_gu, *old])),
            [
                whole(buf_full),
                pl.BlockSpec((1, width, tile), lambda i, s: (early(i), 0, 0)),
                pl.BlockSpec((1, packed, tile), lambda i, s: (early(i), 0, 0)),
                pl.BlockSpec((1, packed, tile), lambda i, s: (early(i), 0, 0)),
                pl.BlockSpec((1, 2 * ffe, wide_chunk), lambda i, s: (jnp.maximum(i - steps, 0), 0, 0)),
                *[anywhere] * len(old),
            ],
            [*[far_out(a) for a in stores[2:]], buf_out],
            [
                slot_block((packed, tile), lambda i: (0, early(i))),
                slot_block((packed, tile), lambda i: (0, early(i))),
                late_block,
            ],
            grid=(steps + width // wide_chunk,),
            scratch=[pltpu.VMEM((packed, 2 * ffe), BF)],
            room=32,
            aliases={1 + len(args) + i: i for i in range(len(old))},
            cost=3 * matmul,
        )
        store = (hidden_t, packed_t, *got[:2])
        returned = to_owners(got[2])
        arrivals.append(arrived)
        before = []
        if tick + 2 == ticks:
            both_slots = lambda shape, place: pl.BlockSpec((micros, *shape), lambda i, s: (0, *place(i)))
            up_tile = lambda i: (i, 0)
            side_tile = lambda i: (0, i)
            stay = lambda i: (0, 0)
            grad_shapes = [sds((width, ffe), BF), sds((width, ffe), BF), sds((ffe, width), BF)]
            earlier = run(
                earlier_kernel,
                (sec, *far([packed_t, store[2], store[3], hidden_t, *arrivals])),
                [
                    both_slots((width, packed), stay),
                    both_slots((packed, tile), side_tile),
                    both_slots((packed, tile), side_tile),
                    both_slots((tile, packed), up_tile),
                    *[whole(buf_full) for _ in arrivals],
                ],
                [far_out(a) for a in grad_shapes],
                [in_block, in_block, down_block],
                grid=(steps,),
                scratch=[pltpu.VMEM((micros, packed, width), BF)],
                cost=6 * matmul,
                room=44,
            )
            before = earlier
        [grad_in] = run(
            functools.partial(combine_bwd_kernel, tick, count),
            (sec, returned, places, *far([grad_normed, gsel, *[c[2] for c in cands], *before])),
            [buf_block, place_block(micro_of), whole(wide_f), whole(row_full)]
            + [whole(row_full)] * count
            + [anywhere] * len(before),
            [row_full],
            [whole(row_full)],
            grid=(col_steps,),
            scratch=[pltpu.VMEM((rows, width), F32)],
            cost=2 * rows * packed * width,
        )
        if tick == 2:
            head_full = sds((width, classes), BF)
            head_args = [part for final in finals for part in (final[0], final[2])]
            [head_term] = run(
                head_sum_kernel,
                (sec, *far(head_args), *far([grad_normed])),
                [*[whole(a) for a in head_args], anywhere],
                [far_out(head_full)],
                [whole(head_full)],
                cost=4 * rows * width * classes,
            )
            head_term, _ = lax.optimization_barrier((head_term, grad_in))
            pieces = to_owners(head_term)
            piece_full = sds((2 * share, classes), BF)
            [piece] = run(
                functools.partial(piece_kernel, experts),
                (sec, pieces),
                [whole(pieces)],
                [piece_full],
                [whole(piece_full)],
            )
            loss_pair = jnp.stack(hi_lo(sum(final[3][0, 0] for final in finals)))
            flat = jnp.concatenate([piece.reshape(-1), loss_pair])
            own = jnp.pad(flat, (0, carry_rows * width - flat.size)).reshape(carry_rows, width)
            others = [lax.ppermute(own, "section", [(sections - 1, t)]) for t in range(sections - 1)]
            carry = jnp.where(section == sections - 1, own, sum(others))
            carry_all = lax.all_gather(carry, plane, axis=0, tiled=False)
        incoming = from_behind(grad_in, "section", -1)

    everyone = lax.all_gather(router_sum, plane, axis=0, tiled=False)
    held = share * classes // width
    router_full, head_full = sds((experts, width), F32), sds((experts, held, width), F32)
    loss_full = sds((experts, 128), F32)
    head_rows, loss_rows = run(
        functools.partial(head_tail_kernel, held),
        (sec, *far([carry_all])),
        [pl.BlockSpec((8, *carry_all.shape[1:]), lambda i, s: (i, 0, 0))],
        [head_full, loss_full],
        [
            pl.BlockSpec((8, held, width), lambda i, s: (i, 0, 0)),
            pl.BlockSpec((8, 128), lambda i, s: (i, 0)),
        ],
        grid=(experts // 8,),
    )
    head_total = head_rows.reshape(width, classes)
    mean_loss = jnp.sum(loss_rows[:, :2]) / (micros * rows * experts)
    [router_rows] = run(
        tail_kernel,
        (sec, *far([everyone])),
        [pl.BlockSpec((*everyone.shape[:2], chunk_b), lambda i, s: (0, 0, i))],
        [router_full],
        [pl.BlockSpec((experts, chunk_b), lambda i, s: (0, i))],
        grid=(width // chunk_b,),
    )
    router_out = router_rows.T[None]

    next_slot = lambda shape, place: pl.BlockSpec((1, *shape), lambda i, s: (1, *place(i)))
    early = lambda i: jnp.minimum(i, steps - 1)
    late = lambda i: jnp.maximum(i - steps, 0)
    down_early = pl.BlockSpec((tile, width), lambda i, s: (early(i), 0))
    act_early = pl.BlockSpec((1, packed, tile), lambda i, s: (early(i), 0, 0))
    in_late = pl.BlockSpec((chunk_b, ffe), lambda i, s: (late(i), 0))
    grad_gate, grad_up, grad_down = run(
        functools.partial(final_kernel, steps),
        (
            sec,
            arrived,
            *far([turned_down, a1, a2, hidden_t, packed_t, *earlier, head_total]),
        ),
        [
            whole(buf_full),
            pl.BlockSpec((1, width, tile), lambda i, s: (early(i), 0, 0)),
            act_early,
            act_early,
            next_slot((tile, packed), lambda i: (early(i), 0)),
            next_slot((chunk_b, packed), lambda i: (late(i), 0)),
            in_late,
            in_late,
            down_early,
            anywhere,
        ],
        grad_shapes,
        [in_late, in_late, down_early],
        grid=(steps + width // chunk_b,),
        scratch=[
            pltpu.VMEM((packed, width), BF),
            pltpu.VMEM((packed, ffe), BF),
            pltpu.VMEM((packed, ffe), BF),
        ],
        cost=4 * matmul,
        room=32,
    )
    return (
        mean_loss,
        head_total,
        router_out,
        grad_gate[None, None],
        grad_up[None, None],
        grad_down[None, None],
    )


def solution(mesh):
    experts = P("section", plane, None, None)
    return jax.shard_map(
        shards,
        mesh=mesh,
        in_specs=(
            P(None, plane, None),
            P("section", None, plane, None),
            P(None, plane),
            P("section", None, None),
            P(),
            experts,
            experts,
            experts,
        ),
        out_specs=(P(), P(), P("section", None, None), experts, experts, experts),
        check_vma=False,
    )
```
